128 devices in a mesh: frow: 8 (over z, core), fcol: 8 (over y_hi, x), chan: 2 (over y_lo).
Axes of the slice: x: 4, y: 4 (y_hi: 2, y_lo: 2; y = y_hi * 2 + y_lo), z: 4, core: 2. Of those that a mesh axis runs over, the one named last changes fastest.
Arguments:
- image_cube: float32 [32, 512, 2048], P('chan', 'frow', 'fcol'), may hold values from -40 to 40
- weights: float32 [3, 512, 2048], P(None, 'frow', 'fcol'), may hold values from 0.5 to 2
Outputs:
- backprojected: float32 [32, 512, 2048], P('chan', 'frow', 'fcol')
- lowrank: float32 [32, 512, 2048], P('chan', 'frow', 'fcol')
The draws below stay inside these ranges and needn't reach their ends.
All inputs are finite; a program needn't handle non-finite values.
Results may differ from the reference program's by a relative error of at most 0.0003.
Values sent between devices are 32-bit elements; how exact they have to be, the bound alone decides.
No kernel may reach another device: no remote copies, remote signals or barrier semaphores. Data moves between devices by JAX's collectives and lax.ppermute only.
A program may use at most 128 MiB of HBM per device.

```python
import math
import jax
import jax.numpy as jnp
import numpy as np
from jax import lax

L = 32
CR = 64
CC = 256
JSWEEPS = 3
NR = 512
NC = 2048
N_FROW = 8
N_FCOL = 8


def draw_image_cube(key, part):
    subkeys = jax.random.split(key, 4)
    noise_part = jax.random.normal(subkeys[0], (L, NR, NC), jnp.float32)
    spectra = 0.7 * jax.random.normal(subkeys[1], (L, 4), jnp.float32)
    sky_maps = jax.random.normal(subkeys[2], (4, NR, NC), jnp.float32)
    rough_part = jax.random.uniform(subkeys[3], (L,), jnp.float32, 0.7, 1.3)
    channel_ramp = 3.0 ** (jnp.arange(L, dtype=jnp.float32) / (L - 1))
    amplitude = channel_ramp * rough_part
    mixture = noise_part + jnp.einsum('lk,kij->lij', spectra, sky_maps)
    return jnp.clip(amplitude[:, None, None] * mixture, -40.0, 40.0).astype(jnp.float32)


def steps_of(stream_key, shape, pieces, smallest, high):
    level, own = 1.0, jax.random.fold_in(stream_key, 6)
    for axis_at, parts in pieces:
        steps = jnp.exp(jax.random.uniform(jax.random.fold_in(own, axis_at), (parts,), jnp.float32, smallest / len(pieces), high / len(pieces)))
        level = level * jnp.repeat(steps, shape[axis_at] // parts).reshape([-1 if axis == axis_at else 1 for axis in range(len(shape))])
    return level


def setup_inputs(seed: int = 0) -> dict:
    arg_keys = jax.random.split(jax.random.key(seed), 3)
    image_cube = draw_image_cube(jax.random.fold_in(arg_keys[2], 71), 0)
    weights = jnp.clip(jnp.exp(math.log(2.0) - 1.3862944 * jax.random.uniform(arg_keys[1], (3, NR, NC), jnp.float32) ** steps_of(arg_keys[1], (3, NR, NC), ((1, 8), (2, 8)), -0.2, 0.2)), 0.5, 2.0)
    return dict(image_cube=image_cube, weights=weights)


filter_taps = (0.0625, 0.25, 0.375, 0.25, 0.0625)
band_levels = (12.0, 4.0, 2.5)
rank_level = 2.0
tiny_value = 1e-30

def smooth(extended, dilation):
    reach_cells = 2 * dilation
    row_count = extended.shape[-2] - 2 * reach_cells
    col_count = extended.shape[-1] - 2 * reach_cells
    across = filter_taps[0] * extended[..., 0:row_count, :]
    for tap_index in range(1, 5):
        offset = tap_index * dilation
        across = across + filter_taps[tap_index] * extended[..., offset:offset + row_count, :]
    result = filter_taps[0] * across[..., 0:col_count]
    for tap_index in range(1, 5):
        offset = tap_index * dilation
        result = result + filter_taps[tap_index] * across[..., offset:offset + col_count]
    return result

def tournament(order_size):
    players = list(range(order_size))
    tables = []
    for round_index in range(order_size - 1):
        first_list = []
        second_list = []
        for slot_index in range(order_size // 2):
            left_one = players[slot_index]
            right_one = players[order_size - 1 - slot_index]
            first_list.append(min(left_one, right_one))
            second_list.append(max(left_one, right_one))
        order_list = np.array(first_list + second_list, np.int32)
        inverse_list = np.argsort(order_list).astype(np.int32)
        tables.append((np.array(first_list, np.int32), np.array(second_list, np.int32), order_list, inverse_list))
        players = [players[0], players[-1]] + players[1:-1]
    return tables

def jacobi(gram_matrix):
    order_size = gram_matrix.shape[0]
    half_size = order_size // 2
    tables = tournament(order_size)
    identity_matrix = jnp.eye(order_size, dtype=gram_matrix.dtype)

    def one_round(matrix, vectors, first_list, second_list, order_list, inverse_list):
        diag_values = jnp.diagonal(matrix)
        left_diag = diag_values[first_list]
        right_diag = diag_values[second_list]
        cross_term = matrix[first_list, second_list]
        gap_value = right_diag - left_diag
        sign_part = jnp.where(gap_value >= 0, 1.0, -1.0)
        tangent = sign_part * 2.0 * cross_term / (jnp.abs(gap_value) + jnp.sqrt(gap_value * gap_value + 4.0 * cross_term * cross_term) + tiny_value)
        cosine = 1.0 / jnp.sqrt(1.0 + tangent * tangent)
        sine_part = tangent * cosine

        def turn_columns(block):
            placed = block[:, order_list]
            left_cols = placed[:, :half_size]
            right_cols = placed[:, half_size:]
            turned = jnp.concatenate([cosine * left_cols - sine_part * right_cols, sine_part * left_cols + cosine * right_cols], axis=1)
            return turned[:, inverse_list]
        matrix = turn_columns(matrix)
        matrix = turn_columns(matrix.T).T
        vectors = turn_columns(vectors)
        return (matrix, vectors)

    def sweep(counter, carried):
        matrix, vectors = carried
        for first_list, second_list, order_list, inverse_list in tables:
            matrix, vectors = one_round(matrix, vectors, first_list, second_list, order_list, inverse_list)
        return (matrix, vectors)
    matrix, vectors = lax.fori_loop(0, JSWEEPS, sweep, (gram_matrix, identity_matrix))
    return (jnp.diagonal(matrix), vectors)

def spectral_map(gram_matrix, threshold):
    values, vectors = jacobi(gram_matrix)
    factors = 1.0 - threshold / jnp.sqrt(jnp.maximum(values, threshold * threshold))
    return jnp.dot(vectors * factors[None, :], vectors.T, precision=lax.Precision.HIGHEST)

def reference(image_cube, weights):
    channels = image_cube.shape[0]
    coarse_one = smooth(jnp.pad(image_cube, ((0, 0), (2, 2), (2, 2))), 1)
    coarse_two = smooth(jnp.pad(coarse_one, ((0, 0), (4, 4), (4, 4))), 2)
    band_list = (image_cube - coarse_one, coarse_one - coarse_two, coarse_two)
    dual_list = []
    for band_index in range(3):
        levels = band_levels[band_index] * weights[band_index]
        totals = lax.optimization_barrier(jnp.sum(band_list[band_index] * band_list[band_index], axis=0))
        dual_list.append(band_list[band_index] * (levels / jnp.sqrt(jnp.maximum(totals, levels * levels))))
    inner_part = smooth(jnp.pad(dual_list[2] - dual_list[1], ((0, 0), (4, 4), (4, 4))), 2)
    summed = dual_list[1] - dual_list[0] + inner_part
    backprojected = dual_list[0] + smooth(jnp.pad(summed, ((0, 0), (2, 2), (2, 2))), 1)
    pixels = CR * CC
    threshold = rank_level * math.sqrt(pixels)
    facets = image_cube.reshape(channels, N_FROW, CR, N_FCOL, CC).transpose(1, 3, 0, 2, 4).reshape(N_FROW * N_FCOL, channels, pixels)

    def project(matrix):
        gram_matrix = jnp.dot(matrix, matrix.T, precision=lax.Precision.HIGHEST)
        mixing = spectral_map(gram_matrix, threshold)
        return jnp.dot(mixing, matrix, precision=lax.Precision.HIGHEST)
    projected = lax.map(project, facets)
    lowrank = projected.reshape(N_FROW, N_FCOL, channels, CR, CC).transpose(2, 0, 3, 1, 4).reshape(channels, N_FROW * CR, N_FCOL * CC)
    return (backprojected, lowrank)
```

```python
import math

import jax
import jax.numpy as jnp
import ml_dtypes
import numpy as np
from jax import lax
from jax.experimental import pallas as pl
from jax.experimental.pallas import tpu as pltpu
from jax.sharding import PartitionSpec as P

JSWEEPS = 3
filter_taps = (0.0625, 0.25, 0.375, 0.25, 0.0625)
band_levels = (12.0, 4.0, 2.5)
rank_level = 2.0
tiny_value = 1e-30

bf16 = jnp.bfloat16
f32 = jnp.float32
ORDER = 32
HALF = 16
OWN = 16
ROWS, COLS = 64, 256
SLOT = 12
PER = 10
EIN, EOUT = 96, 80
WIDE = 384
GRAM_SCALE = float(2.0**32)


def band_matrix(size, dilation):
    out = np.zeros((size, size), np.float64)
    for tap_index, tap in enumerate(filter_taps):
        offset = (tap_index - 2) * dilation
        out += tap * np.eye(size, size, offset)
    return out


def picked(matrix, out_ids, in_ids):
    size = matrix.shape[0]
    out_ok = (out_ids >= 0) & (out_ids < size)
    in_ok = (in_ids >= 0) & (in_ids < size)
    part = matrix[np.clip(out_ids, 0, size - 1)][:, np.clip(in_ids, 0, size - 1)]
    return part * out_ok[:, None] * in_ok[None, :]


def stencil_tables():
    none = -(10**6)
    rows_f, cols_f1, cols_f2, rows_b1, rows_b2, cols_b1, cols_b2 = ([] for _ in range(7))
    for place in range(3):
        a1, a2 = band_matrix(3 * ROWS, 1), band_matrix(3 * ROWS, 2)
        base = place * ROWS
        ein = np.concatenate([base + np.arange(64), base + 64 + np.arange(16), base - 16 + np.arange(16)])
        eout = np.concatenate([base + np.arange(64), base + 64 + np.arange(8), base - 8 + np.arange(8)])
        own = base + np.arange(64)
        fwd = np.concatenate([picked(a1, eout, ein), picked(a2 @ a1, eout, ein)], 0)
        rows_f.append(np.concatenate([fwd, fwd], 1))
        one, two = picked(a1, own, eout), picked(a1 @ a2, own, eout)
        rows_b1.append(np.concatenate([one, one], 1))
        rows_b2.append(np.concatenate([two, two], 1))
        a1, a2 = band_matrix(3 * COLS, 1), band_matrix(3 * COLS, 2)
        base = place * COLS
        right, left = base + COLS + np.arange(SLOT), base - SLOT + np.arange(SLOT)
        pad = np.full(WIDE - COLS - 2 * SLOT, none)
        cin = np.concatenate([base + np.arange(COLS), right, left, pad])
        reach = SLOT // 2
        keep_r = np.where(np.arange(SLOT) < reach, right, none)
        keep_l = np.where(np.arange(SLOT) >= reach, left, none)
        cout = np.concatenate([base + np.arange(COLS), keep_r, keep_l, pad])
        own = base + np.arange(COLS)
        for store, mat in ((cols_f1, a1), (cols_f2, a2 @ a1)):
            part = picked(mat, cout, cin).T
            store.append(np.concatenate([part, part], 0))
        for store, mat in ((cols_b1, a1), (cols_b2, a1 @ a2)):
            part = picked(mat, own, cout).T
            store.append(np.concatenate([part, part], 0))
    return [np.stack(t).astype(ml_dtypes.bfloat16) for t in (rows_f, cols_f1, cols_f2, rows_b1, rows_b2, cols_b1, cols_b2)]


def jacobi_tables():
    players = list(range(ORDER))
    rounds = ORDER - 1
    ints = np.zeros((rounds, 40, 128), np.int32)
    floats = np.zeros((rounds, 16, 128), np.float32)
    for k in range(rounds):
        top = np.array(players[:HALF])
        bottom = np.array([players[ORDER - 1 - i] for i in range(HALF)])
        ints[k, 0:16] = top[:, None]
        ints[k, 16:32] = bottom[:, None]
        partner = np.arange(128)
        partner[top], partner[bottom] = bottom, top
        ints[k, 32:40] = partner[None]
        side = np.zeros(128, np.float32)
        side[top], side[bottom] = 1.0, -1.0
        least = np.zeros(128, np.float32)
        swapped = np.where(top < bottom, 0.0, 1.2e-38)
        least[top], least[bottom] = swapped, swapped
        floats[k, 0:8] = side[None]
        floats[k, 8:16] = least[None]
        players = [players[0], players[-1]] + players[1:-1]
    return ints, floats


def split(x):
    high = x.astype(bf16)
    return high, (x - high.astype(f32)).astype(bf16)


def mm(a, b):
    return jnp.dot(a, b, preferred_element_type=f32)


def pack_kernel(where_ref, x_ref, w_ref, left_ref, right_ref, mine_ref, other_ref):
    chan = where_ref[2]
    lane = lax.broadcasted_iota(jnp.int32, (ROWS, 128), 1)
    for group in range(2):
        low = jnp.zeros((ROWS, 128), f32)
        high = jnp.zeros((ROWS, 128), f32)
        for k in range(PER):
            slot = group * PER + k
            if slot >= OWN + 3:
                break
            tile0 = x_ref[slot, :, 0:128] if slot < OWN else w_ref[slot - OWN, :, 0:128]
            tile1 = x_ref[slot, :, 128:256] if slot < OWN else w_ref[slot - OWN, :, 128:256]
            here = (lane >= SLOT * k) & (lane < SLOT * (k + 1))
            low = jnp.where(here, pltpu.roll(tile0, SLOT * k, 1) if k else tile0, low)
            high = jnp.where(here, pltpu.roll(tile1, (SLOT * k + SLOT) % 128, 1), high)
        left_ref[group] = low
        right_ref[group] = high
    for out_ref, start in ((mine_ref, chan * 32), (other_ref, (1 - chan) * 32)):
        for r in range(4):
            rows = pl.ds(pl.multiple_of(start + 8 * r, 8), 8)
            for c in range(2):
                block = x_ref[8 * c : 8 * c + 8, rows, :]
                out_ref[8 * r : 8 * r + 8, 8 * c : 8 * c + 8, :] = jnp.swapaxes(block, 0, 1)


def gram_kernel(where_ref, own_ref, peer_ref, out_ref):
    first_chan = where_ref[2] == 0
    total = jnp.zeros((64, 64), f32)
    for r in range(0, 32, 4):
        parts = []
        for j in range(4):
            own, peer = own_ref[r + j], peer_ref[r + j]
            both = jnp.concatenate([jnp.where(first_chan, own, peer), jnp.where(first_chan, peer, own)], 0)
            high, low = split(both)
            parts.append(jnp.concatenate([high, low], 0))
        tall = jnp.concatenate(parts, 1)
        total += lax.dot_general(tall, tall, (((1,), (1,)), ((), ())), preferred_element_type=f32)
    gram = (total[0:32, 0:32] + total[32:64, 32:64]) + (total[0:32, 32:64] + total[32:64, 0:32])
    out_ref[...] = jnp.concatenate([gram, jnp.zeros((32, 96), f32)], 1)


def halo_tile(tile_r, tile_l, k):
    lane = lax.broadcasted_iota(jnp.int32, tile_r.shape, 1)
    moved_r = pltpu.roll(tile_r, 128 - SLOT * k, 1) if k else tile_r
    moved_l = pltpu.roll(tile_l, (SLOT + 128 - SLOT * k) % 128, 1) if k != 1 else tile_l
    return jnp.where(lane < SLOT, moved_r, moved_l)


def forward_kernel(where_ref, x_ref, below_ref, above_ref, pr_ref, pl_ref, rows_ref, c1_ref, c2_ref, b_ref, t_ref, ):
    rmat = rows_ref[0]
    for c in range(OWN):
        group, k = c // PER, c % PER
        side = halo_tile(pr_ref[group], pl_ref[group], k)
        side_b = halo_tile(below_ref[OWN + group, :, 0:128], below_ref[OWN + group, :, 128:256], k)
        side_a = halo_tile(above_ref[OWN + group, :, 0:128], above_ref[OWN + group, :, 128:256], k)
        wide = jnp.concatenate(
            [
                jnp.concatenate([x_ref[c], side], 1),
                jnp.concatenate([below_ref[c], side_b], 1),
                jnp.concatenate([above_ref[c], side_a], 1),
            ],
            0,
        )
        high, low = split(wide)
        y = mm(rmat, jnp.concatenate([high, low], 0))
        high, low = split(y)
        z1 = mm(jnp.concatenate([high[:EOUT], low[:EOUT]], 1), c1_ref[0])
        z2 = mm(jnp.concatenate([high[EOUT:], low[EOUT:]], 1), c2_ref[0])
        inner = jnp.concatenate([wide[0:72], wide[88:96]], 0)
        b0, b1 = inner - z1, z1 - z2
        b_ref[c, 0] = b0
        b_ref[c, 1] = b1
        b_ref[c, 2] = z2
        for i, band in enumerate((b0, b1, z2)):
            if c == 0:
                t_ref[i] = band * band
            else:
                t_ref[i] += band * band


def backward_kernel(where_ref, b_ref, t_ref, u_ref, w_ref, below_ref, above_ref, pr_ref, pl_ref,
                    r1_ref, r2_ref, c1_ref, c2_ref, out_ref, f_ref):
    for i in range(3):
        slot = OWN + i
        group, k = slot // PER, slot % PER
        side = halo_tile(pr_ref[group], pl_ref[group], k)
        side_b = halo_tile(below_ref[OWN + group, 0:8, 0:128], below_ref[OWN + group, 0:8, 128:256], k)
        side_a = halo_tile(above_ref[OWN + group, 8:16, 0:128], above_ref[OWN + group, 8:16, 128:256], k)
        weight = jnp.concatenate(
            [
                jnp.concatenate([w_ref[i], side], 1),
                jnp.concatenate([below_ref[18 + i, 0:8], side_b], 1),
                jnp.concatenate([above_ref[18 + i, 8:16], side_a], 1),
            ],
            0,
        )
        level = band_levels[i] * weight
        total = t_ref[i] + u_ref[i]
        f_ref[i] = level * lax.rsqrt(jnp.maximum(jnp.maximum(total, level * level), 1e-30))
    for c in range(OWN):
        d0 = b_ref[c, 0] * f_ref[0]
        d1 = b_ref[c, 1] * f_ref[1]
        d2 = b_ref[c, 2] * f_ref[2]
        high, low = split(d1 - d0)
        y1 = mm(r1_ref[0], jnp.concatenate([high, low], 0))
        high, low = split(d2 - d1)
        y2 = mm(r2_ref[0], jnp.concatenate([high, low], 0))
        high, low = split(y1)
        z = mm(jnp.concatenate([high, low], 1), c1_ref[0])
        high, low = split(y2)
        z += mm(jnp.concatenate([high, low], 1), c2_ref[0])
        out_ref[c] = d0[0:ROWS, 0:COLS] + z


def take(x, ids):
    return jnp.take_along_axis(x, ids, axis=1)


def rotation(gap, cross2, least):
    square = gap * gap + (cross2 * cross2 + 1e-37)
    root = square * lax.rsqrt(square) + tiny_value * GRAM_SCALE
    base = jnp.abs(gap) + root
    inverse = lax.rsqrt(base * base + cross2 * cross2)
    signed = jnp.where(gap >= least, cross2, -cross2)
    return base * inverse, signed * inverse


def sublane_sum(v):
    v = v + pltpu.roll(v, 4, 0)
    v = v + pltpu.roll(v, 2, 0)
    return v + pltpu.roll(v, 1, 0)


def one_round(k, state, ints, floats):
    lane = lax.broadcasted_iota(jnp.int32, (8, 128), 1)
    sub = lax.broadcasted_iota(jnp.int32, (8, 128), 0)
    tops, bottoms = state[:2], state[2:]
    top_ids = (ints[k, 0:8], ints[k, 8:16])
    bottom_ids = (ints[k, 16:24], ints[k, 24:32])
    partner = ints[k, 32:40]
    side, least = floats[k, 0:8], floats[k, 8:16]
    moved_t = [take(v, partner) for v in tops]
    moved_b = [take(v, partner) for v in bottoms]
    by_row = []
    gap = cross = None
    for h in range(2):
        t, b, gt, gb, ti, bi = tops[h], bottoms[h], moved_t[h], moved_b[h], top_ids[h], bottom_ids[h]
        x = take(t, bi)
        by_row.append(rotation(take(b, bi) - take(t, ti), x + x, jnp.where(ti < bi, 0.0, 1.2e-38)))
        on_t, on_b = ti == lane, bi == lane
        part_g = jnp.where(on_t, gb - t, jnp.where(on_b, b - gt, 0.0))
        part_x = jnp.where(on_b, t, jnp.where(on_t, gt, 0.0))
        gap = part_g if gap is None else gap + part_g
        cross = part_x if cross is None else cross + part_x
    gap, cross = sublane_sum(gap), sublane_sum(cross)
    cosine, sine = rotation(gap, cross + cross, least)
    in_gram = lane < ORDER
    cosine = jnp.where(in_gram, cosine, 1.0)
    sine = jnp.where(in_gram, -side * sine, 0.0)
    new_t, new_b = [], []
    for h in range(2):
        c, s = by_row[h]
        t = cosine * tops[h] + sine * moved_t[h]
        b = cosine * bottoms[h] + sine * moved_b[h]
        new_t.append(c * t - s * b)
        new_b.append(s * t + c * b)
    (ta, tb), (ba, bb) = new_t, new_b
    down_a, down_b, first_b = pltpu.roll(ta, 1, 0), pltpu.roll(tb, 1, 0), pltpu.roll(ba, 1, 0)
    up_a, up_b = pltpu.roll(ba, 7, 0), pltpu.roll(bb, 7, 0)
    return (
        jnp.where(sub == 0, ta, jnp.where(sub == 1, first_b, down_a)),
        jnp.where(sub == 0, down_a, down_b),
        jnp.where(sub == 7, up_b, up_a),
        jnp.where(sub == 7, tb, up_b),
    )


def jacobi_kernel(threshold, g_ref, h_ref, ints, floats, out_ref):
    lane = lax.broadcasted_iota(jnp.int32, (8, 128), 1)
    gram = (g_ref[...] + h_ref[...]) * GRAM_SCALE
    labels = [ints[0, 8 * i : 8 * i + 8] for i in range(4)]
    rows = [gram[i : i + 1] for i in range(16)] + [gram[31 - i : 32 - i] for i in range(16)]
    state = tuple(
        jnp.where(lane - ORDER == labels[i], 1.0, jnp.concatenate(rows[8 * i : 8 * i + 8], 0)) for i in range(4)
    )

    def sweep(_, state):
        return lax.fori_loop(0, ORDER - 1, lambda k, s: one_round(k, s, ints, floats), state)

    state = lax.fori_loop(0, JSWEEPS, sweep, state)
    factors = []
    for i in range(4):
        values = take(state[i], labels[i]) * (1.0 / GRAM_SCALE)
        factors.append(1.0 - threshold / jnp.sqrt(jnp.maximum(values, threshold * threshold)))
    whole = jnp.concatenate(state, 0)
    scaled = jnp.concatenate(factors, 0) * whole
    mixing = lax.dot_general(
        scaled, whole, (((0,), (0,)), ((), ())), precision=lax.Precision.HIGHEST, preferred_element_type=f32
    )
    out_ref[...] = pltpu.roll(mixing[ORDER : 2 * ORDER], 128 - ORDER, 1)


def apply_kernel(where_ref, m_ref, mine_ref, other_ref, near_ref, far_ref, out_ref):
    chan = where_ref[2]
    own = m_ref[pl.ds(pl.multiple_of(chan * OWN, OWN), OWN), :]
    first = own[:, 0:16]
    second = own[:, 16:32]
    zero_chan = chan == 0
    mix = jnp.concatenate([jnp.where(zero_chan, first, second), jnp.where(zero_chan, second, first)], 1)
    high, low = split(mix)
    left = jnp.concatenate([high, high, low], 1)
    blank = jnp.zeros_like(left)
    left = jnp.concatenate([jnp.concatenate([left, blank], 1), jnp.concatenate([blank, left], 1)], 0)
    for own_ref, peer_ref, start in ((mine_ref, near_ref, chan * 32), (other_ref, far_ref, (1 - chan) * 32)):
        for r in range(0, 32, 8):
            pieces = []
            for j in range(0, 8, 2):
                stack = []
                for q in range(2):
                    both = jnp.concatenate([own_ref[r + j + q], peer_ref[r + j + q]], 0)
                    high, low = split(both)
                    stack += [high, low, high]
                pieces.append(mm(left, jnp.concatenate(stack, 0)).reshape(2, OWN, COLS))
            block = jnp.concatenate(pieces, 0)
            rows = pl.ds(pl.multiple_of(start + r, 8), 8)
            for c in range(2):
                out_ref[8 * c : 8 * c + 8, rows, :] = jnp.swapaxes(block[:, 8 * c : 8 * c + 8, :], 0, 1)


ROWS_F, COLS_F1, COLS_F2, ROWS_B1, ROWS_B2, COLS_B1, COLS_B2 = stencil_tables()
INTS, FLOATS = jacobi_tables()


def whole(shape):
    return pl.BlockSpec(shape, lambda i, where, n=len(shape): (0,) * n)


def by_row(table):
    return pl.BlockSpec((1, *table.shape[1:]), lambda i, where: (where[0], 0, 0))


def by_col(table):
    return pl.BlockSpec((1, *table.shape[1:]), lambda i, where: (where[1], 0, 0))


def call(kernel, name, where, args, specs, outs, scratch=(), cost=None):
    return pl.pallas_call(
        kernel,
        out_shape=[jax.ShapeDtypeStruct(s, f32) for s in outs],
        grid_spec=pltpu.PrefetchScalarGridSpec(
            num_scalar_prefetch=1,
            grid=(1,),
            in_specs=[whole(a.shape) if s is None else s for a, s in zip(args, specs)],
            out_specs=[whole(s) for s in outs],
            scratch_shapes=list(scratch),
        ),
        compiler_params=pltpu.CompilerParams(vmem_limit_bytes=50 * 2**20),
        cost_estimate=cost,
        name=name,
    )(where, *args)


def shards(x, w):
    frow, fcol, chan = (lax.axis_index(a) for a in ("frow", "fcol", "chan"))
    last_r, last_c = lax.axis_size("frow") - 1, lax.axis_size("fcol") - 1

    def place(i, last):
        return jnp.where(i == 0, 0, jnp.where(i == last, 2, 1))

    where = jnp.stack([place(frow, last_r), place(fcol, last_c), chan]).astype(jnp.int32)
    up = [(i, i + 1) for i in range(7)]
    down = [(i + 1, i) for i in range(7)]
    swap = [(0, 1), (1, 0)]
    tile = (2, ROWS, 128)
    half = (32, OWN, COLS)
    left, right, mine, other = call(
        pack_kernel, "pack", where, (x, w), (None, None), (tile, tile, half, half)
    )
    near = lax.ppermute(other, "chan", swap)
    from_right = lax.ppermute(left, "fcol", down)
    from_left = lax.ppermute(right, "fcol", up)
    far = lax.ppermute(mine, "chan", swap)
    sides = jnp.concatenate([from_right, from_left], 2)

    def edge(rows):
        return jnp.concatenate([x[:, rows], sides[:, rows], w[:, rows]], 0)

    below = lax.ppermute(edge(slice(0, 16)), "frow", down)
    above = lax.ppermute(edge(slice(48, 64)), "frow", up)
    (gram,) = call(gram_kernel, "gram", where, (mine, near), (None, None), ((ORDER, 128),))
    gram_peer = lax.ppermute(gram, "chan", swap)
    bands, totals = call(
        forward_kernel,
        "forward",
        where,
        (x, below, above, from_right, from_left, ROWS_F, COLS_F1, COLS_F2),
        (None,) * 5 + (by_row(ROWS_F), by_col(COLS_F1), by_col(COLS_F2)),
        ((OWN, 3, EOUT, WIDE), (3, EOUT, WIDE)),
    )
    totals_peer = lax.ppermute(totals, "chan", swap)
    threshold = rank_level * math.sqrt(ROWS * COLS)
    mixing = pl.pallas_call(
        lambda *refs: jacobi_kernel(threshold, *refs),
        out_shape=jax.ShapeDtypeStruct((ORDER, 128), f32),
        name="jacobi",
    )(gram, gram_peer, INTS, FLOATS)
    (back,) = call(
        backward_kernel,
        "backward",
        where,
        (bands, totals, totals_peer, w, below, above, from_right, from_left, ROWS_B1, ROWS_B2, COLS_B1, COLS_B2),
        (None,) * 8 + (by_row(ROWS_B1), by_row(ROWS_B2), by_col(COLS_B1), by_col(COLS_B2)),
        ((OWN, ROWS, COLS),),
        (pltpu.VMEM((3, EOUT, WIDE), f32),),
    )
    (low,) = call(
        apply_kernel, "apply", where, (mixing, mine, other, near, far), (None,) * 5, ((OWN, ROWS, COLS),)
    )
    return back, low


def solution(mesh):
    return jax.shard_map(
        shards,
        mesh=mesh,
        in_specs=(P("chan", "frow", "fcol"), P(None, "frow", "fcol")),
        out_specs=(P("chan", "frow", "fcol"), P("chan", "frow", "fcol")),
        check_vma=False,
    )
```

```python
import math

import jax
import jax.numpy as jnp
import ml_dtypes
import numpy as np
from jax import lax
from jax.experimental import pallas as pl
from jax.experimental.pallas import tpu as pltpu
from jax.sharding import PartitionSpec as P

JSWEEPS = 3
filter_taps = (0.0625, 0.25, 0.375, 0.25, 0.0625)
band_levels = (12.0, 4.0, 2.5)
rank_level = 2.0
tiny_value = 1e-30

bf16 = jnp.bfloat16
f32 = jnp.float32
ORDER = 32
HALF = 16
OWN = 16
ROWS, COLS = 64, 256
SLOT = 12
PER = 10
EIN, EOUT = 96, 80
WIDE = 384
GRAM_SCALE = float(2.0**32)
VFIRST = 24
CB = 8


def band_matrix(size, dilation):
    out = np.zeros((size, size), np.float64)
    for tap_index, tap in enumerate(filter_taps):
        offset = (tap_index - 2) * dilation
        out += tap * np.eye(size, size, offset)
    return out


def picked(matrix, out_ids, in_ids):
    size = matrix.shape[0]
    out_ok = (out_ids >= 0) & (out_ids < size)
    in_ok = (in_ids >= 0) & (in_ids < size)
    part = matrix[np.clip(out_ids, 0, size - 1)][:, np.clip(in_ids, 0, size - 1)]
    return part * out_ok[:, None] * in_ok[None, :]


def stencil_tables():
    none = -(10**6)
    rows_f, cols_f1, cols_f2, rows_b1, rows_b2, cols_b1, cols_b2 = ([] for _ in range(7))
    for place in range(3):
        a1, a2 = band_matrix(3 * ROWS, 1), band_matrix(3 * ROWS, 2)
        base = place * ROWS
        ein = np.concatenate([base + np.arange(64), base + 64 + np.arange(16), base - 16 + np.arange(16)])
        eout = np.concatenate([base + np.arange(64), base + 64 + np.arange(8), base - 8 + np.arange(8)])
        own = base + np.arange(64)
        fwd = np.concatenate([picked(a1, eout, ein), picked(a2 @ a1, eout, ein)], 0)
        rows_f.append(np.concatenate([fwd, fwd], 1))
        one, two = picked(a1, own, eout), picked(a1 @ a2, own, eout)
        rows_b1.append(np.concatenate([one, one], 1))
        rows_b2.append(np.concatenate([two, two], 1))
        a1, a2 = band_matrix(3 * COLS, 1), band_matrix(3 * COLS, 2)
        base = place * COLS
        right, left = base + COLS + np.arange(SLOT), base - SLOT + np.arange(SLOT)
        pad = np.full(WIDE - COLS - 2 * SLOT, none)
        cin = np.concatenate([base + np.arange(COLS), right, left, pad])
        reach = SLOT // 2
        keep_r = np.where(np.arange(SLOT) < reach, right, none)
        keep_l = np.where(np.arange(SLOT) >= reach, left, none)
        cout = np.concatenate([base + np.arange(COLS), keep_r, keep_l, pad])
        own = base + np.arange(COLS)
        for store, mat in ((cols_f1, a1), (cols_f2, a2 @ a1)):
            store.append(picked(mat, cout, cin).T)
        for store, mat in ((cols_b1, a1), (cols_b2, a1 @ a2)):
            store.append(picked(mat, own, cout).T)

    def merged(parts, width):
        padded = [np.pad(np.stack(p), ((0, 0), (0, 0), (0, width - p[0].shape[1]))) for p in parts]
        return np.concatenate(padded, 1).astype(ml_dtypes.bfloat16)

    return merged((cols_f1, cols_f2, rows_f), WIDE), merged((cols_b1, cols_b2, rows_b1, rows_b2), COLS)


def jacobi_tables():
    players = list(range(ORDER))
    least = np.zeros((ORDER - 1, HALF, 128), np.float32)
    for k in range(ORDER - 1):
        for i in range(HALF):
            least[k, i] = 0.0 if players[i] < players[ORDER - 1 - i] else 1.2e-38
        players = [players[0], players[-1]] + players[1:-1]
    return least


def split(x):
    high = x.astype(bf16)
    return high, (x - high.astype(f32)).astype(bf16)


def mm(a, b):
    return jnp.dot(a, b, preferred_element_type=f32)


def cut_kernel(where_ref, x_ref, w_ref, half_ref, even_ref, odd_ref, sems):
    start = pl.multiple_of((1 - where_ref[2]) * 32, 32)
    own = pl.multiple_of(where_ref[2] * 32, 32)
    copies = [
        (x_ref.at[:, pl.ds(start, 32), :], half_ref.at[:, 0:32, :]),
        (x_ref.at[:, pl.ds(own, 8), :], half_ref.at[:, 32:40, :]),
    ]
    for out_ref, parity in ((even_ref, 1 - where_ref[3]), (odd_ref, where_ref[3])):
        rows = pl.ds(pl.multiple_of(parity * 48, 16), 16)
        copies.append((x_ref.at[:, rows, :], out_ref.at[0:OWN]))
        copies.append((w_ref.at[:, rows, :], out_ref.at[OWN : OWN + 3]))
    copies = [pltpu.make_async_copy(a, b, sems.at[i]) for i, (a, b) in enumerate(copies)]
    for copy in copies:
        copy.start()
    for copy in copies:
        copy.wait()


def pack_rows(tiles, count, even_ref, odd_ref, at, parity):
    lane = lax.broadcasted_iota(jnp.int32, (count, 128), 1)
    for group in range(2):
        low = jnp.zeros((count, 128), f32)
        high = jnp.zeros((count, 128), f32)
        for k in range(PER):
            slot = group * PER + k
            if slot >= OWN + 3:
                break
            tile0, tile1 = tiles(slot)
            here = (lane >= SLOT * k) & (lane < SLOT * (k + 1))
            low = jnp.where(here, pltpu.roll(tile0, SLOT * k, 1) if k else tile0, low)
            high = jnp.where(here, pltpu.roll(tile1, (SLOT * k + SLOT) % 128, 1), high)
        even_ref[group, at : at + count] = jnp.where(parity == 0, high, low)
        odd_ref[group, at : at + count] = jnp.where(parity == 0, low, high)


def pack_kernel(where_ref, x_ref, w_ref, even_ref, odd_ref, mine_ref, other_ref, held, sems):
    chan = where_ref[2]
    copies = [
        pltpu.make_async_copy(x_ref.at[4 * i : 4 * i + 4], held.at[4 * i : 4 * i + 4], sems.at[i]) for i in range(4)
    ]
    copies.append(pltpu.make_async_copy(w_ref, held.at[OWN : OWN + 3], sems.at[4]))
    for copy in copies:
        copy.start()

    def tiles(slot):
        if slot % 4 == 0:
            copies[slot // 4].wait()
        return held[slot, :, 0:128], held[slot, :, 128:256]

    pack_rows(tiles, ROWS, even_ref, odd_ref, 0, where_ref[4])
    for out_ref, start in ((mine_ref, chan * 32), (other_ref, (1 - chan) * 32)):
        for r in range(4):
            rows = pl.ds(pl.multiple_of(start + 8 * r, 8), 8)
            for c in range(2):
                block = held[8 * c : 8 * c + 8, rows, :]
                out_ref[8 * r : 8 * r + 8, 8 * c : 8 * c + 8, :] = jnp.swapaxes(block, 0, 1)


def pack_halo_kernel(where_ref, old_e, old_o, rows_e, rows_o, even_ref, odd_ref):
    even_ref[:, 0:ROWS] = old_e[:, 0:ROWS]
    odd_ref[:, 0:ROWS] = old_o[:, 0:ROWS]
    upper = where_ref[3] == 0
    for at, flip in ((ROWS, False), (ROWS + 16, True)):

        def tiles(slot, flip=flip):
            one, two = (rows_o, rows_e) if flip else (rows_e, rows_o)
            both = jnp.where(upper, one[slot], two[slot])
            return both[:, 0:128], both[:, 128:256]

        pack_rows(tiles, 16, even_ref, odd_ref, at, where_ref[4])


def gram_kernel(where_ref, own_ref, peer_ref, send_ref, near_ref):
    first_chan = where_ref[2] == 0
    for r in range(5):
        for c in range(2):
            block = peer_ref[8 * c : 8 * c + 8, 8 * r : 8 * r + 8, :]
            near_ref[8 * r : 8 * r + 8, 8 * c : 8 * c + 8, :] = jnp.swapaxes(block, 0, 1)
    total = jnp.zeros((64, 64), f32)
    for r in range(0, 32, 4):
        parts = []
        for j in range(4):
            own, peer = own_ref[r + j], near_ref[r + j]
            both = jnp.concatenate([jnp.where(first_chan, own, peer), jnp.where(first_chan, peer, own)], 0)
            high, low = split(both)
            parts.append(jnp.concatenate([high, low], 0))
        tall = jnp.concatenate(parts, 1)
        total += lax.dot_general(tall, tall, (((1,), (1,)), ((), ())), preferred_element_type=f32)
    gram = (total[0:32, 0:32] + total[32:64, 32:64]) + (total[0:32, 32:64] + total[32:64, 0:32])
    send_ref[...] = jnp.concatenate([gram, jnp.zeros((32, 96), f32)], 1)


def sorted_pair(parity, even, odd):
    return jnp.where(parity == 0, even, odd), jnp.where(parity == 0, odd, even)


def doubled(tables, at, out_ref):
    out_ref[0:WIDE] = tables[at : at + WIDE]
    out_ref[WIDE:] = tables[at : at + WIDE]


def halo_tile(tile_r, tile_l, k):
    lane = lax.broadcasted_iota(jnp.int32, tile_r.shape, 1)
    moved_r = pltpu.roll(tile_r, 128 - SLOT * k, 1) if k else tile_r
    moved_l = pltpu.roll(tile_l, (SLOT + 128 - SLOT * k) % 128, 1) if k != 1 else tile_l
    return jnp.where(lane < SLOT, moved_r, moved_l)


def forward_kernel(where_ref, x_ref, re_ref, ro_ref, ce_ref, co_ref, rmat, c1_ref, c2_ref, bands, totals, c0, wide_ref, s_ref):
    for j in range(CB):
        c = c0 + j
        group, k = c // PER, c % PER
        right, left = sorted_pair(where_ref[4], ce_ref[group], co_ref[group])
        below, above = sorted_pair(where_ref[3], re_ref[c], ro_ref[c])
        side = halo_tile(right, left, k)
        wide = jnp.concatenate([jnp.concatenate([x_ref[c], below, above], 0), side], 1)
        wide_ref[j, 0:72] = wide[0:72]
        wide_ref[j, 72:80] = wide[88:96]
        high, low = split(wide)
        y = mm(rmat, jnp.concatenate([high, low], 0))
        high, low = split(y)
        rows = slice(j * EOUT, (j + 1) * EOUT)
        s_ref[0, rows, 0:WIDE] = high[:EOUT]
        s_ref[0, rows, WIDE:] = low[:EOUT]
        s_ref[1, rows, 0:WIDE] = high[EOUT:]
        s_ref[1, rows, WIDE:] = low[EOUT:]
    z1 = mm(s_ref[0], c1_ref[...])
    z2 = mm(s_ref[1], c2_ref[...])
    for j in range(CB):
        rows = slice(j * EOUT, (j + 1) * EOUT)
        one, two = z1[rows], z2[rows]
        b0, b1 = wide_ref[j] - one, one - two
        bands[j, 0] = b0
        bands[j, 1] = b1
        bands[j, 2] = two
        for i, band in enumerate((b0, b1, two)):
            if c0 + j == 0:
                totals[i] = band * band
            else:
                totals[i] += band * band


def forward_steps(where_ref, x_ref, re_ref, ro_ref, ce_ref, co_ref, cols_ref, rows_ref,
                  b_ref, t_ref, wide_ref, s_ref, totals, d1_ref, d2_ref):
    @pl.when(pl.program_id(0) == 0)
    def _():
        doubled(cols_ref.at[0], 0, d1_ref)
        doubled(cols_ref.at[0], WIDE, d2_ref)

    for step in range(OWN // CB):

        @pl.when(pl.program_id(0) == step)
        def _():
            forward_kernel(where_ref, x_ref, re_ref, ro_ref, ce_ref, co_ref, rows_ref[0, 2 * WIDE :, 0 : 2 * EIN], d1_ref, d2_ref,
                           b_ref, totals, step * CB, wide_ref, s_ref)

    @pl.when(pl.program_id(0) == OWN // CB - 1)
    def _():
        lane = lax.broadcasted_iota(jnp.int32, (EOUT, 128), 1)
        packed = totals[0, :, COLS:]
        for i in range(3):
            t_ref[i * EOUT : (i + 1) * EOUT] = totals[i, :, 0:COLS]
            if i:
                packed = jnp.where(lane < 24 * i, packed, pltpu.roll(totals[i, :, COLS:], 24 * i, 1))
        t_ref[3 * EOUT :] = jnp.concatenate([packed[0 : EOUT // 2], packed[EOUT // 2 :]], 1)


def band_factors(where_ref, t_ref, u_ref, w_ref, re_ref, ro_ref, ce_ref, co_ref, f_ref):
    packed = t_ref[3 * EOUT :] + u_ref[3 * EOUT :]
    packed = jnp.concatenate([packed[:, 0:128], packed[:, 128:256]], 0)
    for i in range(3):
        slot = OWN + i
        group, k = slot // PER, slot % PER
        right, left = sorted_pair(where_ref[4], ce_ref[group], co_ref[group])
        below, above = sorted_pair(where_ref[3], re_ref[slot], ro_ref[slot])
        side = halo_tile(right, left, k)
        side = jnp.concatenate([side[0:72], side[88:96]], 0)
        weight = jnp.concatenate([w_ref[i], below[0:8], above[8:16]], 0)
        weight = jnp.concatenate([weight, side], 1)
        level = band_levels[i] * weight
        rows = slice(i * EOUT, (i + 1) * EOUT)
        outer = pltpu.roll(packed, 128 - 24 * i, 1) if i else packed
        total = jnp.concatenate([t_ref[rows] + u_ref[rows], outer], 1)
        f_ref[i] = level * lax.rsqrt(jnp.maximum(jnp.maximum(total, level * level), 1e-30))


def backward_kernel(where_ref, b_ref, t_ref, u_ref, w_ref, re_ref, ro_ref, ce_ref, co_ref,
                    cols_ref, rows_ref, out_ref, f_ref, s_ref, e1_ref, e2_ref):
    @pl.when(pl.program_id(0) == 0)
    def _():
        band_factors(where_ref, t_ref, u_ref, w_ref, re_ref, ro_ref, ce_ref, co_ref, f_ref)
        doubled(cols_ref.at[0], 0, e1_ref)
        doubled(cols_ref.at[0], WIDE, e2_ref)

    for j in range(CB):
        d0 = b_ref[j, 0] * f_ref[0]
        d1 = b_ref[j, 1] * f_ref[1]
        d2 = b_ref[j, 2] * f_ref[2]
        rows = slice(j * EOUT, (j + 1) * EOUT)
        for i, diff in enumerate((d1 - d0, d2 - d1)):
            high, low = split(diff)
            s_ref[i, rows, 0:WIDE] = high
            s_ref[i, rows, WIDE:] = low
        out_ref[j] = d0[0:ROWS, 0:COLS]
    r1 = rows_ref[0, 2 * WIDE : 2 * WIDE + ROWS, 0 : 2 * EOUT]
    r2 = rows_ref[0, 2 * WIDE + ROWS :, 0 : 2 * EOUT]
    y1 = mm(s_ref[0], e1_ref[...])
    y2 = mm(s_ref[1], e2_ref[...])
    for j in range(CB):
        rows = slice(j * EOUT, (j + 1) * EOUT)
        high, low = split(y1[rows])
        z = mm(r1, jnp.concatenate([high, low], 0))
        high, low = split(y2[rows])
        z += mm(r2, jnp.concatenate([high, low], 0))
        out_ref[j] += z


def rotation(gap, cross2, least):
    cross4 = cross2 * cross2
    square = gap * gap + (cross4 + 1e-37)
    root = square * lax.rsqrt(square) + tiny_value * GRAM_SCALE
    base = jnp.abs(gap) + root
    inverse = lax.rsqrt(base * base + cross4)
    signed = jnp.where(gap >= least, cross2, -cross2)
    return base * inverse, signed * inverse


def rotations(top, bottom, cross, least):
    both = [rotation(b - t, x + x, e) for t, b, x, e in zip(top, bottom, cross, least)]
    return tuple(p[0] for p in both), tuple(p[1] for p in both)


def shift(top, bottom):
    sub = lax.broadcasted_iota(jnp.int32, (8, 128), 0)
    (ta, tb), (ba, bb) = top, bottom
    down_a, down_b, first_b = pltpu.roll(ta, 1, 0), pltpu.roll(tb, 1, 0), pltpu.roll(ba, 1, 0)
    up_a, up_b = pltpu.roll(ba, 7, 0), pltpu.roll(bb, 7, 0)
    return (
        (jnp.where(sub == 0, ta, jnp.where(sub == 1, first_b, down_a)), jnp.where(sub == 0, down_a, down_b)),
        (jnp.where(sub == 7, up_b, up_a), jnp.where(sub == 7, tb, up_b)),
    )


def turn(cosine, sine, top, bottom):
    return shift(
        tuple(c * t - s * b for c, s, t, b in zip(cosine, sine, top, bottom)),
        tuple(s * t + c * b for c, s, t, b in zip(cosine, sine, top, bottom)),
    )


def dots(left, right):
    return [jnp.broadcast_to(jnp.sum(a * b, 1, keepdims=True), (8, 128)) for a, b in zip(left, right)]


def one_round(state, least):
    kt, kb, ut, ub = state
    c, s = rotations(dots(kt, ut), dots(kb, ub), dots(kt, ub), least)
    return turn(c, s, kt, kb) + turn(c, s, ut, ub)


def two_rounds(state, least, least_next):
    kt, kb, ut, ub = state
    top, bottom, cross = dots(kt, ut), dots(kb, ub), dots(kt, ub)
    kt_t, kb_t = shift(kt, kt)[0], shift(kb, kb)[0]
    ut_b, ub_b = shift(ut, ut)[1], shift(ub, ub)[1]
    quads = zip(dots(kt_t, ut_b), dots(kt_t, ub_b), dots(kb_t, ut_b), dots(kb_t, ub_b))
    c, s = rotations(top, bottom, cross, least)
    new_top, new_bottom = [], []
    for ci, si, t, b, x in zip(c, s, top, bottom, cross):
        cc, ss, mixed = ci * ci, si * si, (2.0 * ci * si) * x
        new_top.append(cc * t + ss * b - mixed)
        new_bottom.append(ss * t + cc * b + mixed)
    new_top, new_bottom = shift(new_top, new_bottom)
    of_t, of_b = shift(c, s), shift(tuple(-v for v in s), c)
    new_cross = [
        at * (ab * tt + bb * tb) + bt * (ab * bt_ + bb * bb_)
        for at, ab, bt, bb, (tt, tb, bt_, bb_) in zip(of_t[0], of_t[1], of_b[0], of_b[1], quads)
    ]
    c2, s2 = rotations(new_top, new_bottom, new_cross, least_next)
    kt, kb = turn(c2, s2, *turn(c, s, kt, kb))
    ut, ub = turn(c2, s2, *turn(c, s, ut, ub))
    return kt, kb, ut, ub


def jacobi_kernel(threshold, g_ref, h_ref, table, out_ref):
    lane = lax.broadcasted_iota(jnp.int32, (8, 128), 1)
    sub = lax.broadcasted_iota(jnp.int32, (8, 128), 0)
    gram = (g_ref[...] + h_ref[...]) * GRAM_SCALE
    rows = [gram[i : i + 1] for i in range(16)] + [gram[31 - i : 32 - i] for i in range(16)]
    k = [jnp.concatenate(rows[8 * i : 8 * i + 8], 0) for i in range(4)]
    u = [jnp.where(lane == label, 1.0, 0.0) for label in (sub, sub + 8, 31 - sub, 23 - sub)]
    state = ((k[0], k[1]), (k[2], k[3]), (u[0], u[1]), (u[2], u[3]))
    total = JSWEEPS * (ORDER - 1)

    def least(m):
        at = lax.rem(m, ORDER - 1)
        return table[at, 0:8], table[at, 8:16]

    state = lax.fori_loop(
        0, total // 2, lambda m, held: two_rounds(held, least(2 * m), least(2 * m + 1)), state
    )
    if total % 2:
        state = one_round(state, least(total - 1))
    kt, kb, ut, ub = state
    factors = []
    for value in dots(kt + kb, ut + ub):
        value = jnp.maximum(value * (1.0 / GRAM_SCALE), threshold * threshold)
        factors.append(1.0 - threshold / jnp.sqrt(value))
    vectors = jnp.concatenate(ut + ub, 0)
    mixing = lax.dot_general(
        jnp.concatenate(factors, 0) * vectors,
        vectors,
        (((0,), (0,)), ((), ())),
        precision=lax.Precision.HIGHEST,
        preferred_element_type=f32,
    )
    out_ref[...] = mixing[0:ORDER]


def apply_kernel(where_ref, m_ref, mine_ref, other_ref, near_ref, far1_ref, far2_ref, out_ref):
    chan = where_ref[2]
    own = m_ref[pl.ds(pl.multiple_of(chan * OWN, OWN), OWN), :]
    first = own[:, 0:16]
    second = own[:, 16:32]
    zero_chan = chan == 0
    mix = jnp.concatenate([jnp.where(zero_chan, first, second), jnp.where(zero_chan, second, first)], 1)
    high, low = split(mix)
    left = jnp.concatenate([high, high, low], 1)
    blank = jnp.zeros_like(left)
    left = jnp.concatenate([jnp.concatenate([left, blank], 1), jnp.concatenate([blank, left], 1)], 0)
    for own_ref, peer_ref, first_row, start, count in (
        (mine_ref, near_ref, 0, chan * 32, 32),
        (other_ref, near_ref.at[32:40], 0, (1 - chan) * 32, 8),
        (other_ref, far1_ref, 8, (1 - chan) * 32, 16),
        (other_ref, far2_ref, 24, (1 - chan) * 32, 8),
    ):
        for r in range(0, count, 8):
            pieces = []
            for j in range(0, 8, 2):
                stack = []
                for q in range(2):
                    both = jnp.concatenate([own_ref[first_row + r + j + q], peer_ref[r + j + q]], 0)
                    high, low = split(both)
                    stack += [high, low, high]
                pieces.append(mm(left, jnp.concatenate(stack, 0)).reshape(2, OWN, COLS))
            block = jnp.concatenate(pieces, 0)
            rows = pl.ds(pl.multiple_of(start + first_row + r, 8), 8)
            for c in range(2):
                out_ref[8 * c : 8 * c + 8, rows, :] = jnp.swapaxes(block[:, 8 * c : 8 * c + 8, :], 0, 1)


FORWARD, BACKWARD = stencil_tables()
LEAST = jacobi_tables()


def whole(shape):
    return pl.BlockSpec(shape, lambda i, where, n=len(shape): (0,) * n)


def at_place(table, axis):
    return pl.BlockSpec((1, *table.shape[1:]), lambda i, where: (where[axis], 0, 0))


def call(kernel, name, where, args, outs, specs=None, out_specs=None, scratch=(), grid=1, vmem=24, us=1.0):
    specs = specs or (None,) * len(args)
    out_specs = out_specs or (None,) * len(outs)
    return pl.pallas_call(
        kernel,
        out_shape=[jax.ShapeDtypeStruct(s, f32) for s in outs],
        grid_spec=pltpu.PrefetchScalarGridSpec(
            num_scalar_prefetch=1,
            grid=(grid,),
            in_specs=[whole(a.shape) if s is None else s for a, s in zip(args, specs)],
            out_specs=[whole(a) if s is None else s for a, s in zip(outs, out_specs)],
            scratch_shapes=list(scratch),
        ),
        compiler_params=pltpu.CompilerParams(vmem_limit_bytes=vmem * 2**20),
        cost_estimate=pl.CostEstimate(flops=0, bytes_accessed=int(us * 3.5e6), transcendentals=0),
        name=name,
    )(where, *args)


def shards(x, w):
    frow, fcol, chan = (lax.axis_index(a) for a in ("frow", "fcol", "chan"))
    last_r, last_c = lax.axis_size("frow") - 1, lax.axis_size("fcol") - 1

    def place(i, last):
        return jnp.where(i == 0, 0, jnp.where(i == last, 2, 1))

    where = jnp.stack([place(frow, last_r), place(fcol, last_c), chan, frow % 2, fcol % 2]).astype(jnp.int32)
    even = [(i, i ^ 1) for i in range(8)]
    odd = [(i, i + 1) for i in range(1, 7, 2)] + [(i + 1, i) for i in range(1, 7, 2)]
    swap = [(0, 1), (1, 0)]
    tile = (2, EIN, 128)
    half = (32, OWN, COLS)
    rim = (OWN + 3, 16, COLS)
    hbm = pl.BlockSpec(memory_space=pltpu.HBM)
    cut, rim_e, rim_o = call(
        cut_kernel,
        "cut",
        where,
        (x, w),
        ((OWN, 40, COLS), rim, rim),
        (hbm, hbm),
        scratch=(pltpu.SemaphoreType.DMA((6,)),),
        vmem=VFIRST,
    )
    near = lax.ppermute(cut, "chan", swap)
    rows_o = lax.ppermute(rim_o, "frow", odd)
    rows_e = lax.ppermute(rim_e, "frow", even)
    late, _ = lax.optimization_barrier((where, cut))
    side_e, side_o, mine, other = call(
        pack_kernel,
        "pack",
        late,
        (x, w),
        (tile, tile, half, half),
        (hbm, hbm),
        scratch=(pltpu.VMEM((OWN + 3, ROWS, COLS), f32), pltpu.SemaphoreType.DMA((5,))),
        us=1.5,
    )
    side_e, side_o = call(
        pack_halo_kernel, "pack_halo", where, (side_e, side_o, rows_e, rows_o), (tile, tile), us=0.7
    )
    cols_o = lax.ppermute(side_o, "fcol", odd)
    own, _ = lax.optimization_barrier((mine, side_o))
    send, near = call(gram_kernel, "gram", where, (own, near), ((ORDER, 128), (40, OWN, COLS)), us=1.2)
    side_e, _ = lax.optimization_barrier((side_e, send))
    cols_e = lax.ppermute(side_e, "fcol", even)
    got = lax.ppermute(send, "chan", swap)
    cols_e, cols_o, got = lax.optimization_barrier((cols_e, cols_o, got))
    steps = OWN // CB
    bands, totals = call(
        forward_steps,
        "forward",
        where,
        (x, rows_e, rows_o, cols_e, cols_o, FORWARD, FORWARD),
        ((OWN, 3, EOUT, WIDE), (3 * EOUT + EOUT // 2, COLS)),
        (None,) * 5 + (at_place(FORWARD, 1), at_place(FORWARD, 0)),
        (pl.BlockSpec((CB, 3, EOUT, WIDE), lambda i, where: (i, 0, 0, 0)), None),
        (
            pltpu.VMEM((CB, EOUT, WIDE), f32),
            pltpu.VMEM((2, CB * EOUT, 2 * WIDE), bf16),
            pltpu.VMEM((3, EOUT, WIDE), f32),
            pltpu.VMEM((2 * WIDE, WIDE), bf16),
            pltpu.VMEM((2 * WIDE, WIDE), bf16),
        ),
        steps,
        us=4.5,
    )
    totals_peer = lax.ppermute(totals, "chan", swap)
    part1, part2, _ = lax.optimization_barrier((mine[8:24], mine[24:32], totals))
    far1 = lax.ppermute(part1, "chan", swap)
    far2 = lax.ppermute(part2, "chan", swap)
    threshold = rank_level * math.sqrt(ROWS * COLS)
    send, _ = lax.optimization_barrier((send, totals))
    (mixing,) = call(
        lambda where_ref, *refs: jacobi_kernel(threshold, *refs),
        "jacobi",
        where,
        (send, got, LEAST),
        ((ORDER, 128),),
        us=8.5,
    )
    (back,) = call(
        backward_kernel,
        "backward",
        where,
        (bands, totals, totals_peer, w, rows_e, rows_o, cols_e, cols_o, BACKWARD, BACKWARD),
        ((OWN, ROWS, COLS),),
        (pl.BlockSpec((CB, 3, EOUT, WIDE), lambda i, where: (i, 0, 0, 0)),)
        + (None,) * 7
        + (at_place(BACKWARD, 1), at_place(BACKWARD, 0)),
        (pl.BlockSpec((CB, ROWS, COLS), lambda i, where: (i, 0, 0)),),
        (
            pltpu.VMEM((3, EOUT, WIDE), f32),
            pltpu.VMEM((2, CB * EOUT, 2 * WIDE), bf16),
            pltpu.VMEM((2 * WIDE, COLS), bf16),
            pltpu.VMEM((2 * WIDE, COLS), bf16),
        ),
        steps,
        us=4.5,
    )
    mixing, back = lax.optimization_barrier((mixing, back))
    (low,) = call(
        apply_kernel, "apply", where, (mixing, mine, other, near, far1, far2), ((OWN, ROWS, COLS),), us=2.4
    )
    return back, low


def solution(mesh):
    return jax.shard_map(
        shards,
        mesh=mesh,
        in_specs=(P("chan", "frow", "fcol"), P(None, "frow", "fcol")),
        out_specs=(P("chan", "frow", "fcol"), P("chan", "frow", "fcol")),
        check_vma=False,
    )
```

```python
import math

import jax
import jax.numpy as jnp
import ml_dtypes
import numpy as np
from jax import lax
from jax.experimental import pallas as pl
from jax.experimental.pallas import tpu as pltpu
from jax.sharding import PartitionSpec as P

JSWEEPS = 3
filter_taps = (0.0625, 0.25, 0.375, 0.25, 0.0625)
band_levels = (12.0, 4.0, 2.5)
rank_level = 2.0
tiny_value = 1e-30

bf16 = jnp.bfloat16
f32 = jnp.float32
ORDER = 32
HALF = 16
OWN = 16
ROWS, COLS = 64, 256
SLOT = 12
PER = 10
EIN, EOUT = 96, 80
WIDE = 384
GRAM_SCALE = float(2.0**32)
CB = 8


def band_matrix(size, dilation):
    out = np.zeros((size, size), np.float64)
    for tap_index, tap in enumerate(filter_taps):
        offset = (tap_index - 2) * dilation
        out += tap * np.eye(size, size, offset)
    return out


def picked(matrix, out_ids, in_ids):
    size = matrix.shape[0]
    out_ok = (out_ids >= 0) & (out_ids < size)
    in_ok = (in_ids >= 0) & (in_ids < size)
    part = matrix[np.clip(out_ids, 0, size - 1)][:, np.clip(in_ids, 0, size - 1)]
    return part * out_ok[:, None] * in_ok[None, :]


def stencil_tables():
    none = -(10**6)
    rows_f, cols_f1, cols_f2, rows_b1, rows_b2, cols_b1, cols_b2 = ([] for _ in range(7))
    for place in range(3):
        a1, a2 = band_matrix(3 * ROWS, 1), band_matrix(3 * ROWS, 2)
        base = place * ROWS
        ein = np.concatenate([base + np.arange(64), base + 64 + np.arange(16), base - 16 + np.arange(16)])
        eout = np.concatenate([base + np.arange(64), base + 64 + np.arange(8), base - 8 + np.arange(8)])
        own = base + np.arange(64)
        fwd = np.concatenate([picked(a1, eout, ein), picked(a2 @ a1, eout, ein)], 0)
        rows_f.append(np.concatenate([fwd, fwd], 1))
        one, two = picked(a1, own, eout), picked(a1 @ a2, own, eout)
        rows_b1.append(np.concatenate([one, one], 1))
        rows_b2.append(np.concatenate([two, two], 1))
        a1, a2 = band_matrix(3 * COLS, 1), band_matrix(3 * COLS, 2)
        base = place * COLS
        right, left = base + COLS + np.arange(SLOT), base - SLOT + np.arange(SLOT)
        pad = np.full(WIDE - COLS - 2 * SLOT, none)
        cin = np.concatenate([base + np.arange(COLS), right, left, pad])
        reach = SLOT // 2
        keep_r = np.where(np.arange(SLOT) < reach, right, none)
        keep_l = np.where(np.arange(SLOT) >= reach, left, none)
        cout = np.concatenate([base + np.arange(COLS), keep_r, keep_l, pad])
        own = base + np.arange(COLS)
        for store, mat in ((cols_f1, a1), (cols_f2, a2 @ a1)):
            store.append(picked(mat, cout, cin).T)
        for store, mat in ((cols_b1, a1), (cols_b2, a1 @ a2)):
            store.append(picked(mat, own, cout).T)

    def merged(parts, width):
        padded = [np.pad(np.stack(p), ((0, 0), (0, 0), (0, width - p[0].shape[1]))) for p in parts]
        return np.concatenate(padded, 1).astype(ml_dtypes.bfloat16)

    return merged((cols_f1, cols_f2, rows_f), WIDE), merged((cols_b1, cols_b2, rows_b1, rows_b2), COLS)


def jacobi_tables():
    players = list(range(ORDER))
    least = np.zeros((ORDER - 1, HALF, 128), np.float32)
    for k in range(ORDER - 1):
        for i in range(HALF):
            least[k, i] = 0.0 if players[i] < players[ORDER - 1 - i] else 1.2e-38
        players = [players[0], players[-1]] + players[1:-1]
    return least


def split(x):
    high = x.astype(bf16)
    return high, (x - high.astype(f32)).astype(bf16)


def mm(a, b):
    return jnp.dot(a, b, preferred_element_type=f32)


def cut_kernel(where_ref, x_ref, half_ref, sems):
    start = pl.multiple_of((1 - where_ref[2]) * 32, 32)
    own = pl.multiple_of(where_ref[2] * 32, 32)
    copies = [
        (x_ref.at[:, pl.ds(start, 32), :], half_ref.at[:, 0:32, :]),
        (x_ref.at[:, pl.ds(own, 8), :], half_ref.at[:, 32:40, :]),
    ]
    copy_all(copies, sems)


def copy_all(copies, sems):
    copies = [pltpu.make_async_copy(a, b, sems.at[i]) for i, (a, b) in enumerate(copies)]
    for copy in copies:
        copy.start()
    for copy in copies:
        copy.wait()


def rim_kernel(where_ref, x_ref, w_ref, even_ref, odd_ref, sems):
    copies = []
    for out_ref, parity in ((even_ref, 1 - where_ref[3]), (odd_ref, where_ref[3])):
        rows = pl.ds(pl.multiple_of(parity * 48, 16), 16)
        copies.append((x_ref.at[:, rows, :], out_ref.at[0:OWN]))
        copies.append((w_ref.at[:, rows, :], out_ref.at[OWN : OWN + 3]))
    copy_all(copies, sems)


def pack_rows(tiles, count, even_ref, odd_ref, at, parity):
    lane = lax.broadcasted_iota(jnp.int32, (count, 128), 1)
    for group in range(2):
        low = jnp.zeros((count, 128), f32)
        high = jnp.zeros((count, 128), f32)
        for k in range(PER):
            slot = group * PER + k
            if slot >= OWN + 3:
                break
            tile0, tile1 = tiles(slot)
            here = (lane >= SLOT * k) & (lane < SLOT * (k + 1))
            low = jnp.where(here, pltpu.roll(tile0, SLOT * k, 1) if k else tile0, low)
            high = jnp.where(here, pltpu.roll(tile1, (SLOT * k + SLOT) % 128, 1), high)
        even_ref[group, at : at + count] = jnp.where(parity == 0, high, low)
        odd_ref[group, at : at + count] = jnp.where(parity == 0, low, high)


def pack_kernel(where_ref, x_ref, w_ref, even_ref, odd_ref, mine_ref, other_ref, held, sems):
    chan = where_ref[2]
    copies = [
        pltpu.make_async_copy(x_ref.at[4 * i : 4 * i + 4], held.at[4 * i : 4 * i + 4], sems.at[i]) for i in range(4)
    ]
    copies.append(pltpu.make_async_copy(w_ref, held.at[OWN : OWN + 3], sems.at[4]))
    for copy in copies:
        copy.start()

    def tiles(slot):
        if slot % 4 == 0:
            copies[slot // 4].wait()
        return held[slot, :, 0:128], held[slot, :, 128:256]

    pack_rows(tiles, ROWS, even_ref, odd_ref, 0, where_ref[4])
    for out_ref, start in ((mine_ref, chan * 32), (other_ref, (1 - chan) * 32)):
        for r in range(4):
            rows = pl.ds(pl.multiple_of(start + 8 * r, 8), 8)
            for c in range(2):
                block = held[8 * c : 8 * c + 8, rows, :]
                out_ref[8 * r : 8 * r + 8, 8 * c : 8 * c + 8, :] = jnp.swapaxes(block, 0, 1)


def pack_halo_kernel(where_ref, old_e, old_o, rows_e, rows_o, even_ref, odd_ref):
    even_ref[:, 0:ROWS] = old_e[:, 0:ROWS]
    odd_ref[:, 0:ROWS] = old_o[:, 0:ROWS]
    upper = where_ref[3] == 0
    for at, flip in ((ROWS, False), (ROWS + 16, True)):

        def tiles(slot, flip=flip):
            one, two = (rows_o, rows_e) if flip else (rows_e, rows_o)
            both = jnp.where(upper, one[slot], two[slot])
            return both[:, 0:128], both[:, 128:256]

        pack_rows(tiles, 16, even_ref, odd_ref, at, where_ref[4])


def gram_kernel(where_ref, own_ref, peer_ref, send_ref, near_ref):
    first_chan = where_ref[2] == 0
    for r in range(5):
        for c in range(2):
            block = peer_ref[8 * c : 8 * c + 8, 8 * r : 8 * r + 8, :]
            near_ref[8 * r : 8 * r + 8, 8 * c : 8 * c + 8, :] = jnp.swapaxes(block, 0, 1)
    total = jnp.zeros((64, 64), f32)
    for r in range(0, 32, 4):
        parts = []
        for j in range(4):
            own, peer = own_ref[r + j], near_ref[r + j]
            both = jnp.concatenate([jnp.where(first_chan, own, peer), jnp.where(first_chan, peer, own)], 0)
            high, low = split(both)
            parts.append(jnp.concatenate([high, low], 0))
        tall = jnp.concatenate(parts, 1)
        total += lax.dot_general(tall, tall, (((1,), (1,)), ((), ())), preferred_element_type=f32)
    gram = (total[0:32, 0:32] + total[32:64, 32:64]) + (total[0:32, 32:64] + total[32:64, 0:32])
    send_ref[...] = jnp.concatenate([gram, jnp.zeros((32, 96), f32)], 1)


def sorted_pair(parity, even, odd):
    return jnp.where(parity == 0, even, odd), jnp.where(parity == 0, odd, even)


def doubled(tables, at, out_ref):
    out_ref[0:WIDE] = tables[at : at + WIDE]
    out_ref[WIDE:] = tables[at : at + WIDE]


def halo_tile(tile_r, tile_l, k):
    lane = lax.broadcasted_iota(jnp.int32, tile_r.shape, 1)
    moved_r = pltpu.roll(tile_r, 128 - SLOT * k, 1) if k else tile_r
    moved_l = pltpu.roll(tile_l, (SLOT + 128 - SLOT * k) % 128, 1) if k != 1 else tile_l
    return jnp.where(lane < SLOT, moved_r, moved_l)


def forward_kernel(where_ref, x_ref, re_ref, ro_ref, ce_ref, co_ref, rmat, c1_ref, c2_ref, bands, totals, c0, wide_ref, s_ref):
    for j in range(CB):
        c = c0 + j
        group, k = c // PER, c % PER
        right, left = sorted_pair(where_ref[4], ce_ref[group], co_ref[group])
        below, above = sorted_pair(where_ref[3], re_ref[c], ro_ref[c])
        side = halo_tile(right, left, k)
        wide = jnp.concatenate([jnp.concatenate([x_ref[c], below, above], 0), side], 1)
        wide_ref[j, 0:72] = wide[0:72]
        wide_ref[j, 72:80] = wide[88:96]
        high, low = split(wide)
        y = mm(rmat, jnp.concatenate([high, low], 0))
        high, low = split(y)
        rows = slice(j * EOUT, (j + 1) * EOUT)
        s_ref[0, rows, 0:WIDE] = high[:EOUT]
        s_ref[0, rows, WIDE:] = low[:EOUT]
        s_ref[1, rows, 0:WIDE] = high[EOUT:]
        s_ref[1, rows, WIDE:] = low[EOUT:]
    z1 = mm(s_ref[0], c1_ref[...])
    z2 = mm(s_ref[1], c2_ref[...])
    for j in range(CB):
        rows = slice(j * EOUT, (j + 1) * EOUT)
        one, two = z1[rows], z2[rows]
        b0, b1 = wide_ref[j] - one, one - two
        bands[j, 0] = b0
        bands[j, 1] = b1
        bands[j, 2] = two
        for i, band in enumerate((b0, b1, two)):
            if c0 + j == 0:
                totals[i] = band * band
            else:
                totals[i] += band * band


def forward_steps(where_ref, x_ref, re_ref, ro_ref, ce_ref, co_ref, cols_ref, rows_ref,
                  b_ref, t_ref, wide_ref, s_ref, totals, d1_ref, d2_ref):
    @pl.when(pl.program_id(0) == 0)
    def _():
        doubled(cols_ref.at[0], 0, d1_ref)
        doubled(cols_ref.at[0], WIDE, d2_ref)

    for step in range(OWN // CB):

        @pl.when(pl.program_id(0) == step)
        def _():
            forward_kernel(where_ref, x_ref, re_ref, ro_ref, ce_ref, co_ref, rows_ref[0, 2 * WIDE :, 0 : 2 * EIN], d1_ref, d2_ref,
                           b_ref, totals, step * CB, wide_ref, s_ref)

    @pl.when(pl.program_id(0) == OWN // CB - 1)
    def _():
        lane = lax.broadcasted_iota(jnp.int32, (EOUT, 128), 1)
        packed = totals[0, :, COLS:]
        for i in range(3):
            t_ref[i * EOUT : (i + 1) * EOUT] = totals[i, :, 0:COLS]
            if i:
                packed = jnp.where(lane < 24 * i, packed, pltpu.roll(totals[i, :, COLS:], 24 * i, 1))
        t_ref[3 * EOUT :] = jnp.concatenate([packed[0 : EOUT // 2], packed[EOUT // 2 :]], 1)


def band_factors(where_ref, t_ref, u_ref, w_ref, re_ref, ro_ref, ce_ref, co_ref, f_ref):
    packed = t_ref[3 * EOUT :] + u_ref[3 * EOUT :]
    packed = jnp.concatenate([packed[:, 0:128], packed[:, 128:256]], 0)
    for i in range(3):
        slot = OWN + i
        group, k = slot // PER, slot % PER
        right, left = sorted_pair(where_ref[4], ce_ref[group], co_ref[group])
        below, above = sorted_pair(where_ref[3], re_ref[slot], ro_ref[slot])
        side = halo_tile(right, left, k)
        side = jnp.concatenate([side[0:72], side[88:96]], 0)
        weight = jnp.concatenate([w_ref[i], below[0:8], above[8:16]], 0)
        weight = jnp.concatenate([weight, side], 1)
        level = band_levels[i] * weight
        rows = slice(i * EOUT, (i + 1) * EOUT)
        outer = pltpu.roll(packed, 128 - 24 * i, 1) if i else packed
        total = jnp.concatenate([t_ref[rows] + u_ref[rows], outer], 1)
        f_ref[i] = level * lax.rsqrt(jnp.maximum(jnp.maximum(total, level * level), 1e-30))


def backward_kernel(where_ref, b_ref, t_ref, u_ref, w_ref, re_ref, ro_ref, ce_ref, co_ref,
                    cols_ref, rows_ref, out_ref, f_ref, s_ref, e1_ref, e2_ref):
    @pl.when(pl.program_id(0) == 0)
    def _():
        band_factors(where_ref, t_ref, u_ref, w_ref, re_ref, ro_ref, ce_ref, co_ref, f_ref)
        doubled(cols_ref.at[0], 0, e1_ref)
        doubled(cols_ref.at[0], WIDE, e2_ref)

    for j in range(CB):
        d0 = b_ref[j, 0] * f_ref[0]
        d1 = b_ref[j, 1] * f_ref[1]
        d2 = b_ref[j, 2] * f_ref[2]
        rows = slice(j * EOUT, (j + 1) * EOUT)
        for i, diff in enumerate((d1 - d0, d2 - d1)):
            high, low = split(diff)
            s_ref[i, rows, 0:WIDE] = high
            s_ref[i, rows, WIDE:] = low
        out_ref[j] = d0[0:ROWS, 0:COLS]
    r1 = rows_ref[0, 2 * WIDE : 2 * WIDE + ROWS, 0 : 2 * EOUT]
    r2 = rows_ref[0, 2 * WIDE + ROWS :, 0 : 2 * EOUT]
    y1 = mm(s_ref[0], e1_ref[...])
    y2 = mm(s_ref[1], e2_ref[...])
    for j in range(CB):
        rows = slice(j * EOUT, (j + 1) * EOUT)
        high, low = split(y1[rows])
        z = mm(r1, jnp.concatenate([high, low], 0))
        high, low = split(y2[rows])
        z += mm(r2, jnp.concatenate([high, low], 0))
        out_ref[j] += z


def rotation(gap, cross2, least):
    cross4 = cross2 * cross2
    square = gap * gap + (cross4 + 1e-37)
    root = square * lax.rsqrt(square) + tiny_value * GRAM_SCALE
    base = jnp.abs(gap) + root
    inverse = lax.rsqrt(base * base + cross4)
    signed = jnp.where(gap >= least, cross2, -cross2)
    return base * inverse, signed * inverse


def rotations(top, bottom, cross, least):
    both = [rotation(b - t, x + x, e) for t, b, x, e in zip(top, bottom, cross, least)]
    return tuple(p[0] for p in both), tuple(p[1] for p in both)


def shift(top, bottom):
    sub = lax.broadcasted_iota(jnp.int32, (8, 128), 0)
    (ta, tb), (ba, bb) = top, bottom
    down_a, down_b, first_b = pltpu.roll(ta, 1, 0), pltpu.roll(tb, 1, 0), pltpu.roll(ba, 1, 0)
    up_a, up_b = pltpu.roll(ba, 7, 0), pltpu.roll(bb, 7, 0)
    return (
        (jnp.where(sub == 0, ta, jnp.where(sub == 1, first_b, down_a)), jnp.where(sub == 0, down_a, down_b)),
        (jnp.where(sub == 7, up_b, up_a), jnp.where(sub == 7, tb, up_b)),
    )


def turn(cosine, sine, top, bottom):
    return shift(
        tuple(c * t - s * b for c, s, t, b in zip(cosine, sine, top, bottom)),
        tuple(s * t + c * b for c, s, t, b in zip(cosine, sine, top, bottom)),
    )


def dots(left, right):
    return [jnp.broadcast_to(jnp.sum(a * b, 1, keepdims=True), (8, 128)) for a, b in zip(left, right)]


def one_round(state, least):
    kt, kb, ut, ub = state
    c, s = rotations(dots(kt, ut), dots(kb, ub), dots(kt, ub), least)
    return turn(c, s, kt, kb) + turn(c, s, ut, ub)


def two_rounds(state, least, least_next):
    kt, kb, ut, ub = state
    top, bottom, cross = dots(kt, ut), dots(kb, ub), dots(kt, ub)
    kt_t, kb_t = shift(kt, kt)[0], shift(kb, kb)[0]
    ut_b, ub_b = shift(ut, ut)[1], shift(ub, ub)[1]
    quads = zip(dots(kt_t, ut_b), dots(kt_t, ub_b), dots(kb_t, ut_b), dots(kb_t, ub_b))
    c, s = rotations(top, bottom, cross, least)
    new_top, new_bottom = [], []
    for ci, si, t, b, x in zip(c, s, top, bottom, cross):
        cc, ss, mixed = ci * ci, si * si, (2.0 * ci * si) * x
        new_top.append(cc * t + ss * b - mixed)
        new_bottom.append(ss * t + cc * b + mixed)
    new_top, new_bottom = shift(new_top, new_bottom)
    of_t, of_b = shift(c, s), shift(tuple(-v for v in s), c)
    new_cross = [
        at * (ab * tt + bb * tb) + bt * (ab * bt_ + bb * bb_)
        for at, ab, bt, bb, (tt, tb, bt_, bb_) in zip(of_t[0], of_t[1], of_b[0], of_b[1], quads)
    ]
    c2, s2 = rotations(new_top, new_bottom, new_cross, least_next)
    kt, kb = turn(c2, s2, *turn(c, s, kt, kb))
    ut, ub = turn(c2, s2, *turn(c, s, ut, ub))
    return kt, kb, ut, ub


def jacobi_kernel(threshold, g_ref, h_ref, table, out_ref):
    lane = lax.broadcasted_iota(jnp.int32, (8, 128), 1)
    sub = lax.broadcasted_iota(jnp.int32, (8, 128), 0)
    gram = (g_ref[...] + h_ref[...]) * GRAM_SCALE
    rows = [gram[i : i + 1] for i in range(16)] + [gram[31 - i : 32 - i] for i in range(16)]
    k = [jnp.concatenate(rows[8 * i : 8 * i + 8], 0) for i in range(4)]
    u = [jnp.where(lane == label, 1.0, 0.0) for label in (sub, sub + 8, 31 - sub, 23 - sub)]
    state = ((k[0], k[1]), (k[2], k[3]), (u[0], u[1]), (u[2], u[3]))
    total = JSWEEPS * (ORDER - 1)

    def least(m):
        at = lax.rem(m, ORDER - 1)
        return table[at, 0:8], table[at, 8:16]

    state = lax.fori_loop(
        0, total // 2, lambda m, held: two_rounds(held, least(2 * m), least(2 * m + 1)), state
    )
    if total % 2:
        state = one_round(state, least(total - 1))
    kt, kb, ut, ub = state
    factors = []
    for value in dots(kt + kb, ut + ub):
        value = jnp.maximum(value * (1.0 / GRAM_SCALE), threshold * threshold)
        factors.append(1.0 - threshold / jnp.sqrt(value))
    vectors = jnp.concatenate(ut + ub, 0)
    mixing = lax.dot_general(
        jnp.concatenate(factors, 0) * vectors,
        vectors,
        (((0,), (0,)), ((), ())),
        precision=lax.Precision.HIGHEST,
        preferred_element_type=f32,
    )
    out_ref[...] = mixing[0:ORDER]


def mixing_left(where_ref, m_ref):
    own = m_ref[pl.ds(pl.multiple_of(where_ref[2] * OWN, OWN), OWN), :]
    first = own[:, 0:16]
    second = own[:, 16:32]
    zero_chan = where_ref[2] == 0
    mix = jnp.concatenate([jnp.where(zero_chan, first, second), jnp.where(zero_chan, second, first)], 1)
    high, low = split(mix)
    left = jnp.concatenate([high, high, low], 1)
    blank = jnp.zeros_like(left)
    return jnp.concatenate([jnp.concatenate([left, blank], 1), jnp.concatenate([blank, left], 1)], 0)


def apply_rows(left, own_ref, peer_ref, out_ref, first_row, count):
    for r in range(0, count, 8):
        pieces = []
        for j in range(0, 8, 2):
            stack = []
            for q in range(2):
                both = jnp.concatenate([own_ref[first_row + r + j + q], peer_ref[r + j + q]], 0)
                high, low = split(both)
                stack += [high, low, high]
            pieces.append(mm(left, jnp.concatenate(stack, 0)).reshape(2, OWN, COLS))
        block = jnp.concatenate(pieces, 0)
        for c in range(2):
            rows = slice(first_row + r, first_row + r + 8)
            out_ref[8 * c : 8 * c + 8, rows, :] = jnp.swapaxes(block[:, 8 * c : 8 * c + 8, :], 0, 1)


def apply_near(where_ref, m_ref, mine_ref, near_ref, out_ref):
    apply_rows(mixing_left(where_ref, m_ref), mine_ref, near_ref, out_ref, 0, 32)


def apply_far(where_ref, m_ref, other_ref, near_ref, far1_ref, far2_ref, done_ref, out_ref):
    left = mixing_left(where_ref, m_ref)
    apply_rows(left, other_ref, near_ref.at[32:40], out_ref, 0, 8)
    apply_rows(left, other_ref, far1_ref, out_ref, 8, 16)
    apply_rows(left, other_ref, far2_ref, out_ref, 24, 8)


FORWARD, BACKWARD = stencil_tables()
LEAST = jacobi_tables()


def whole(shape):
    return pl.BlockSpec(shape, lambda i, where, n=len(shape): (0,) * n)


def at_place(table, axis):
    return pl.BlockSpec((1, *table.shape[1:]), lambda i, where: (where[axis], 0, 0))


def call(kernel, name, where, args, outs, specs=None, out_specs=None, scratch=(), grid=1, vmem=24, us=1.0, alias=None):
    specs = specs or (None,) * len(args)
    out_specs = out_specs or (None,) * len(outs)
    return pl.pallas_call(
        kernel,
        out_shape=[jax.ShapeDtypeStruct(s, f32) for s in outs],
        grid_spec=pltpu.PrefetchScalarGridSpec(
            num_scalar_prefetch=1,
            grid=(grid,),
            in_specs=[whole(a.shape) if s is None else s for a, s in zip(args, specs)],
            out_specs=[whole(a) if s is None else s for a, s in zip(outs, out_specs)],
            scratch_shapes=list(scratch),
        ),
        compiler_params=pltpu.CompilerParams(vmem_limit_bytes=vmem * 2**20),
        cost_estimate=pl.CostEstimate(flops=0, bytes_accessed=int(us * 3.5e6), transcendentals=0),
        input_output_aliases=alias or {},
        name=name,
    )(where, *args)


def shards(x, w):
    frow, fcol, chan = (lax.axis_index(a) for a in ("frow", "fcol", "chan"))
    last_r, last_c = lax.axis_size("frow") - 1, lax.axis_size("fcol") - 1

    def place(i, last):
        return jnp.where(i == 0, 0, jnp.where(i == last, 2, 1))

    where = jnp.stack([place(frow, last_r), place(fcol, last_c), chan, frow % 2, fcol % 2]).astype(jnp.int32)
    even = [(i, i ^ 1) for i in range(8)]
    odd = [(i, i + 1) for i in range(1, 7, 2)] + [(i + 1, i) for i in range(1, 7, 2)]
    swap = [(0, 1), (1, 0)]
    tile = (2, EIN, 128)
    half = (32, OWN, COLS)
    rim = (OWN + 3, 16, COLS)
    hbm = pl.BlockSpec(memory_space=pltpu.HBM)
    (cut,) = call(
        cut_kernel, "cut", where, (x,), ((OWN, 40, COLS),), (hbm,), scratch=(pltpu.SemaphoreType.DMA((2,)),), us=0.6
    )
    near = lax.ppermute(cut, "chan", swap)
    later, _ = lax.optimization_barrier((where, cut))
    rim_e, rim_o = call(
        rim_kernel, "rim", later, (x, w), (rim, rim), (hbm, hbm), scratch=(pltpu.SemaphoreType.DMA((4,)),), us=0.6
    )
    rows_o = lax.ppermute(rim_o, "frow", odd)
    rows_e = lax.ppermute(rim_e, "frow", even)
    late, _ = lax.optimization_barrier((where, rim_e))
    side_e, side_o, mine, other = call(
        pack_kernel,
        "pack",
        late,
        (x, w),
        (tile, tile, half, half),
        (hbm, hbm),
        scratch=(pltpu.VMEM((OWN + 3, ROWS, COLS), f32), pltpu.SemaphoreType.DMA((5,))),
        us=1.5,
    )
    side_e, side_o = call(
        pack_halo_kernel, "pack_halo", where, (side_e, side_o, rows_e, rows_o), (tile, tile), us=0.7
    )
    cols_o = lax.ppermute(side_o, "fcol", odd)
    own, _ = lax.optimization_barrier((mine, side_o))
    send, near = call(gram_kernel, "gram", where, (own, near), ((ORDER, 128), (40, OWN, COLS)), us=1.2)
    side_e, _ = lax.optimization_barrier((side_e, send))
    cols_e = lax.ppermute(side_e, "fcol", even)
    got = lax.ppermute(send, "chan", swap)
    cols_e, cols_o, got = lax.optimization_barrier((cols_e, cols_o, got))
    steps = OWN // CB
    bands, totals = call(
        forward_steps,
        "forward",
        where,
        (x, rows_e, rows_o, cols_e, cols_o, FORWARD, FORWARD),
        ((OWN, 3, EOUT, WIDE), (3 * EOUT + EOUT // 2, COLS)),
        (None,) * 5 + (at_place(FORWARD, 1), at_place(FORWARD, 0)),
        (pl.BlockSpec((CB, 3, EOUT, WIDE), lambda i, where: (i, 0, 0, 0)), None),
        (
            pltpu.VMEM((CB, EOUT, WIDE), f32),
            pltpu.VMEM((2, CB * EOUT, 2 * WIDE), bf16),
            pltpu.VMEM((3, EOUT, WIDE), f32),
            pltpu.VMEM((2 * WIDE, WIDE), bf16),
            pltpu.VMEM((2 * WIDE, WIDE), bf16),
        ),
        steps,
        us=4.5,
    )
    totals_peer = lax.ppermute(totals, "chan", swap)
    part1, part2, _ = lax.optimization_barrier((mine[8:24], mine[24:32], totals))
    far1 = lax.ppermute(part1, "chan", swap)
    far2 = lax.ppermute(part2, "chan", swap)
    threshold = rank_level * math.sqrt(ROWS * COLS)
    send, _ = lax.optimization_barrier((send, totals))
    (mixing,) = call(
        lambda where_ref, *refs: jacobi_kernel(threshold, *refs),
        "jacobi",
        where,
        (send, got, LEAST),
        ((ORDER, 128),),
        us=8.5,
    )
    (low,) = call(
        apply_near,
        "apply_near",
        where,
        (mixing, mine, near),
        ((OWN, ROWS, COLS),),
        None,
        (pl.BlockSpec((OWN, 32, COLS), lambda i, where: (0, where[2], 0)),),
        us=1.2,
    )
    totals_peer, low = lax.optimization_barrier((totals_peer, low))
    (back,) = call(
        backward_kernel,
        "backward",
        where,
        (bands, totals, totals_peer, w, rows_e, rows_o, cols_e, cols_o, BACKWARD, BACKWARD),
        ((OWN, ROWS, COLS),),
        (pl.BlockSpec((CB, 3, EOUT, WIDE), lambda i, where: (i, 0, 0, 0)),)
        + (None,) * 7
        + (at_place(BACKWARD, 1), at_place(BACKWARD, 0)),
        (pl.BlockSpec((CB, ROWS, COLS), lambda i, where: (i, 0, 0)),),
        (
            pltpu.VMEM((3, EOUT, WIDE), f32),
            pltpu.VMEM((2, CB * EOUT, 2 * WIDE), bf16),
            pltpu.VMEM((2 * WIDE, COLS), bf16),
            pltpu.VMEM((2 * WIDE, COLS), bf16),
        ),
        steps,
        us=4.5,
    )
    low, back = lax.optimization_barrier((low, back))
    (low,) = call(
        apply_far,
        "apply_far",
        where,
        (mixing, other, near, far1, far2, low),
        ((OWN, ROWS, COLS),),
        (None,) * 5 + (hbm,),
        (pl.BlockSpec((OWN, 32, COLS), lambda i, where: (0, 1 - where[2], 0)),),
        us=1.2,
        alias={6: 0},
    )
    return back, low


def solution(mesh):
    return jax.shard_map(
        shards,
        mesh=mesh,
        in_specs=(P("chan", "frow", "fcol"), P(None, "frow", "fcol")),
        out_specs=(P("chan", "frow", "fcol"), P("chan", "frow", "fcol")),
        check_vma=False,
    )
```

```python
import math

import jax
import jax.numpy as jnp
import ml_dtypes
import numpy as np
from jax import lax
from jax.experimental import pallas as pl
from jax.experimental.pallas import tpu as pltpu
from jax.sharding import PartitionSpec as P

JSWEEPS = 3
filter_taps = (0.0625, 0.25, 0.375, 0.25, 0.0625)
band_levels = (12.0, 4.0, 2.5)
rank_level = 2.0
tiny_value = 1e-30

bf16 = jnp.bfloat16
f32 = jnp.float32
ORDER = 32
HALF = 16
OWN = 16
ROWS, COLS = 64, 256
SLOT = 12
PER = 10
EIN, EOUT = 96, 80
WIDE = 384
GRAM_SCALE = float(2.0**32)
CB = 16


def band_matrix(size, dilation):
    out = np.zeros((size, size), np.float64)
    for tap_index, tap in enumerate(filter_taps):
        offset = (tap_index - 2) * dilation
        out += tap * np.eye(size, size, offset)
    return out


def picked(matrix, out_ids, in_ids):
    size = matrix.shape[0]
    out_ok = (out_ids >= 0) & (out_ids < size)
    in_ok = (in_ids >= 0) & (in_ids < size)
    part = matrix[np.clip(out_ids, 0, size - 1)][:, np.clip(in_ids, 0, size - 1)]
    return part * out_ok[:, None] * in_ok[None, :]


def stencil_tables():
    none = -(10**6)
    rows_f, cols_f1, cols_f2, rows_b1, rows_b2, cols_b1, cols_b2 = ([] for _ in range(7))
    for place in range(3):
        a1, a2 = band_matrix(3 * ROWS, 1), band_matrix(3 * ROWS, 2)
        base = place * ROWS
        ein = np.concatenate([base + np.arange(64), base + 64 + np.arange(16), base - 16 + np.arange(16)])
        eout = np.concatenate([base + np.arange(64), base + 64 + np.arange(8), base - 8 + np.arange(8)])
        own = base + np.arange(64)
        fwd = np.concatenate([picked(a1, eout, ein), picked(a2 @ a1, eout, ein)], 0)
        rows_f.append(np.concatenate([fwd, fwd], 1))
        one, two = picked(a1, own, eout), picked(a1 @ a2, own, eout)
        rows_b1.append(np.concatenate([one, one], 1))
        rows_b2.append(np.concatenate([two, two], 1))
        a1, a2 = band_matrix(3 * COLS, 1), band_matrix(3 * COLS, 2)
        base = place * COLS
        right, left = base + COLS + np.arange(SLOT), base - SLOT + np.arange(SLOT)
        pad = np.full(WIDE - COLS - 2 * SLOT, none)
        cin = np.concatenate([base + np.arange(COLS), right, left, pad])
        reach = SLOT // 2
        keep_r = np.where(np.arange(SLOT) < reach, right, none)
        keep_l = np.where(np.arange(SLOT) >= reach, left, none)
        cout = np.concatenate([base + np.arange(COLS), keep_r, keep_l, pad])
        own = base + np.arange(COLS)
        for store, mat in ((cols_f1, a1), (cols_f2, a2 @ a1)):
            store.append(picked(mat, cout, cin).T)
        for store, mat in ((cols_b1, a1), (cols_b2, a1 @ a2)):
            store.append(picked(mat, own, cout).T)

    def merged(parts, width):
        padded = [np.pad(np.stack(p), ((0, 0), (0, 0), (0, width - p[0].shape[1]))) for p in parts]
        return np.concatenate(padded, 1).astype(ml_dtypes.bfloat16)

    return merged((cols_f1, cols_f2, rows_f), WIDE), merged((cols_b1, cols_b2, rows_b1, rows_b2), COLS)


def jacobi_tables():
    players = list(range(ORDER))
    least = np.zeros((ORDER - 1, HALF, 128), np.float32)
    for k in range(ORDER - 1):
        for i in range(HALF):
            least[k, i] = 0.0 if players[i] < players[ORDER - 1 - i] else 1.2e-38
        players = [players[0], players[-1]] + players[1:-1]
    return least


def split(x):
    high = x.astype(bf16)
    return high, (x - high.astype(f32)).astype(bf16)


def mm(a, b):
    return jnp.dot(a, b, preferred_element_type=f32)


def cut_kernel(where_ref, x_ref, half_ref, sems):
    start = pl.multiple_of((1 - where_ref[2]) * 32, 32)
    own = pl.multiple_of(where_ref[2] * 32, 32)
    copies = [
        (x_ref.at[:, pl.ds(start, 32), :], half_ref.at[:, 0:32, :]),
        (x_ref.at[:, pl.ds(own, 8), :], half_ref.at[:, 32:40, :]),
    ]
    copy_all(copies, sems)


def copy_all(copies, sems):
    copies = [pltpu.make_async_copy(a, b, sems.at[i]) for i, (a, b) in enumerate(copies)]
    for copy in copies:
        copy.start()
    for copy in copies:
        copy.wait()


def rim_kernel(where_ref, x_ref, w_ref, even_ref, odd_ref, sems):
    copies = []
    for out_ref, parity in ((even_ref, 1 - where_ref[3]), (odd_ref, where_ref[3])):
        rows = pl.ds(pl.multiple_of(parity * 48, 16), 16)
        copies.append((x_ref.at[:, rows, :], out_ref.at[0:OWN]))
        copies.append((w_ref.at[:, rows, :], out_ref.at[OWN : OWN + 3]))
    copy_all(copies, sems)


def pack_rows(tiles, count, even_ref, odd_ref, at, parity):
    lane = lax.broadcasted_iota(jnp.int32, (count, 128), 1)
    for group in range(2):
        low = jnp.zeros((count, 128), f32)
        high = jnp.zeros((count, 128), f32)
        for k in range(PER):
            slot = group * PER + k
            if slot >= OWN + 3:
                break
            tile0, tile1 = tiles(slot)
            here = (lane >= SLOT * k) & (lane < SLOT * (k + 1))
            low = jnp.where(here, pltpu.roll(tile0, SLOT * k, 1) if k else tile0, low)
            high = jnp.where(here, pltpu.roll(tile1, (SLOT * k + SLOT) % 128, 1), high)
        even_ref[group, at : at + count] = jnp.where(parity == 0, high, low)
        odd_ref[group, at : at + count] = jnp.where(parity == 0, low, high)


def pack_kernel(where_ref, x_ref, w_ref, even_ref, odd_ref, mine_ref, other_ref, held, sems):
    chan = where_ref[2]
    copies = [
        pltpu.make_async_copy(x_ref.at[4 * i : 4 * i + 4], held.at[4 * i : 4 * i + 4], sems.at[i]) for i in range(4)
    ]
    copies.append(pltpu.make_async_copy(w_ref, held.at[OWN : OWN + 3], sems.at[4]))
    for copy in copies:
        copy.start()

    def tiles(slot):
        if slot % 4 == 0:
            copies[slot // 4].wait()
        return held[slot, :, 0:128], held[slot, :, 128:256]

    pack_rows(tiles, ROWS, even_ref, odd_ref, 0, where_ref[4])
    for out_ref, start in ((mine_ref, chan * 32), (other_ref, (1 - chan) * 32)):
        for r in range(4):
            rows = pl.ds(pl.multiple_of(start + 8 * r, 8), 8)
            for c in range(2):
                block = held[8 * c : 8 * c + 8, rows, :]
                out_ref[8 * r : 8 * r + 8, 8 * c : 8 * c + 8, :] = jnp.swapaxes(block, 0, 1)


def pack_halo_kernel(where_ref, old_e, old_o, rows_e, rows_o, even_ref, odd_ref):
    even_ref[:, 0:ROWS] = old_e[:, 0:ROWS]
    odd_ref[:, 0:ROWS] = old_o[:, 0:ROWS]
    upper = where_ref[3] == 0
    for at, flip in ((ROWS, False), (ROWS + 16, True)):

        def tiles(slot, flip=flip):
            one, two = (rows_o, rows_e) if flip else (rows_e, rows_o)
            both = jnp.where(upper, one[slot], two[slot])
            return both[:, 0:128], both[:, 128:256]

        pack_rows(tiles, 16, even_ref, odd_ref, at, where_ref[4])


def gram_kernel(where_ref, own_ref, peer_ref, send_ref, near_ref):
    first_chan = where_ref[2] == 0
    for r in range(5):
        for c in range(2):
            block = peer_ref[8 * c : 8 * c + 8, 8 * r : 8 * r + 8, :]
            near_ref[8 * r : 8 * r + 8, 8 * c : 8 * c + 8, :] = jnp.swapaxes(block, 0, 1)
    total = jnp.zeros((64, 64), f32)
    for r in range(0, 32, 4):
        parts = []
        for j in range(4):
            own, peer = own_ref[r + j], near_ref[r + j]
            both = jnp.concatenate([jnp.where(first_chan, own, peer), jnp.where(first_chan, peer, own)], 0)
            high, low = split(both)
            parts.append(jnp.concatenate([high, low], 0))
        tall = jnp.concatenate(parts, 1)
        total += lax.dot_general(tall, tall, (((1,), (1,)), ((), ())), preferred_element_type=f32)
    gram = (total[0:32, 0:32] + total[32:64, 32:64]) + (total[0:32, 32:64] + total[32:64, 0:32])
    send_ref[...] = jnp.concatenate([gram, jnp.zeros((32, 96), f32)], 1)


def sorted_pair(parity, even, odd):
    return jnp.where(parity == 0, even, odd), jnp.where(parity == 0, odd, even)


def doubled(tables, at, out_ref):
    out_ref[0:WIDE] = tables[at : at + WIDE]
    out_ref[WIDE:] = tables[at : at + WIDE]


def halo_tile(tile_r, tile_l, k):
    lane = lax.broadcasted_iota(jnp.int32, tile_r.shape, 1)
    moved_r = pltpu.roll(tile_r, 128 - SLOT * k, 1) if k else tile_r
    moved_l = pltpu.roll(tile_l, (SLOT + 128 - SLOT * k) % 128, 1) if k != 1 else tile_l
    return jnp.where(lane < SLOT, moved_r, moved_l)


def forward_kernel(where_ref, x_ref, re_ref, ro_ref, ce_ref, co_ref, rmat, c1_ref, c2_ref, bands, totals, c0, wide_ref, s_ref):
    for j in range(CB):
        c = c0 + j
        group, k = c // PER, c % PER
        right, left = sorted_pair(where_ref[4], ce_ref[group], co_ref[group])
        below, above = sorted_pair(where_ref[3], re_ref[c], ro_ref[c])
        side = halo_tile(right, left, k)
        wide = jnp.concatenate([jnp.concatenate([x_ref[c], below, above], 0), side], 1)
        wide_ref[j, 0:72] = wide[0:72]
        wide_ref[j, 72:80] = wide[88:96]
        high, low = split(wide)
        y = mm(rmat, jnp.concatenate([high, low], 0))
        high, low = split(y)
        rows = slice(j * EOUT, (j + 1) * EOUT)
        s_ref[0, rows, 0:WIDE] = high[:EOUT]
        s_ref[0, rows, WIDE:] = low[:EOUT]
        s_ref[1, rows, 0:WIDE] = high[EOUT:]
        s_ref[1, rows, WIDE:] = low[EOUT:]
    z1 = mm(s_ref[0], c1_ref[...])
    z2 = mm(s_ref[1], c2_ref[...])
    for j in range(CB):
        rows = slice(j * EOUT, (j + 1) * EOUT)
        one, two = z1[rows], z2[rows]
        b0, b1 = wide_ref[j] - one, one - two
        bands[j, 0] = b0
        bands[j, 1] = b1
        bands[j, 2] = two
        for i, band in enumerate((b0, b1, two)):
            if c0 + j == 0:
                totals[i] = band * band
            else:
                totals[i] += band * band


def forward_steps(where_ref, x_ref, re_ref, ro_ref, ce_ref, co_ref, cols_ref, rows_ref,
                  b_ref, t_ref, wide_ref, s_ref, totals, d1_ref, d2_ref):
    @pl.when(pl.program_id(0) == 0)
    def _():
        doubled(cols_ref.at[0], 0, d1_ref)
        doubled(cols_ref.at[0], WIDE, d2_ref)

    for step in range(OWN // CB):

        @pl.when(pl.program_id(0) == step)
        def _():
            forward_kernel(where_ref, x_ref, re_ref, ro_ref, ce_ref, co_ref, rows_ref[0, 2 * WIDE :, 0 : 2 * EIN], d1_ref, d2_ref,
                           b_ref, totals, step * CB, wide_ref, s_ref)

    @pl.when(pl.program_id(0) == OWN // CB - 1)
    def _():
        lane = lax.broadcasted_iota(jnp.int32, (EOUT, 128), 1)
        packed = totals[0, :, COLS:]
        for i in range(3):
            t_ref[i * EOUT : (i + 1) * EOUT] = totals[i, :, 0:COLS]
            if i:
                packed = jnp.where(lane < 24 * i, packed, pltpu.roll(totals[i, :, COLS:], 24 * i, 1))
        t_ref[3 * EOUT :] = jnp.concatenate([packed[0 : EOUT // 2], packed[EOUT // 2 :]], 1)


def band_factors(where_ref, t_ref, u_ref, w_ref, re_ref, ro_ref, ce_ref, co_ref, f_ref):
    packed = t_ref[3 * EOUT :] + u_ref[3 * EOUT :]
    packed = jnp.concatenate([packed[:, 0:128], packed[:, 128:256]], 0)
    for i in range(3):
        slot = OWN + i
        group, k = slot // PER, slot % PER
        right, left = sorted_pair(where_ref[4], ce_ref[group], co_ref[group])
        below, above = sorted_pair(where_ref[3], re_ref[slot], ro_ref[slot])
        side = halo_tile(right, left, k)
        side = jnp.concatenate([side[0:72], side[88:96]], 0)
        weight = jnp.concatenate([w_ref[i], below[0:8], above[8:16]], 0)
        weight = jnp.concatenate([weight, side], 1)
        level = band_levels[i] * weight
        rows = slice(i * EOUT, (i + 1) * EOUT)
        outer = pltpu.roll(packed, 128 - 24 * i, 1) if i else packed
        total = jnp.concatenate([t_ref[rows] + u_ref[rows], outer], 1)
        f_ref[i] = level * lax.rsqrt(jnp.maximum(jnp.maximum(total, level * level), 1e-30))


def backward_kernel(where_ref, b_ref, t_ref, u_ref, w_ref, re_ref, ro_ref, ce_ref, co_ref,
                    cols_ref, rows_ref, out_ref, f_ref, s_ref, e1_ref, e2_ref):
    @pl.when(pl.program_id(0) == 0)
    def _():
        band_factors(where_ref, t_ref, u_ref, w_ref, re_ref, ro_ref, ce_ref, co_ref, f_ref)
        doubled(cols_ref.at[0], 0, e1_ref)
        doubled(cols_ref.at[0], WIDE, e2_ref)

    for j in range(CB):
        d0 = b_ref[j, 0] * f_ref[0]
        d1 = b_ref[j, 1] * f_ref[1]
        d2 = b_ref[j, 2] * f_ref[2]
        rows = slice(j * EOUT, (j + 1) * EOUT)
        for i, diff in enumerate((d1 - d0, d2 - d1)):
            high, low = split(diff)
            s_ref[i, rows, 0:WIDE] = high
            s_ref[i, rows, WIDE:] = low
        out_ref[j] = d0[0:ROWS, 0:COLS]
    r1 = rows_ref[0, 2 * WIDE : 2 * WIDE + ROWS, 0 : 2 * EOUT]
    r2 = rows_ref[0, 2 * WIDE + ROWS :, 0 : 2 * EOUT]
    y1 = mm(s_ref[0], e1_ref[...])
    y2 = mm(s_ref[1], e2_ref[...])
    for j in range(CB):
        rows = slice(j * EOUT, (j + 1) * EOUT)
        high, low = split(y1[rows])
        z = mm(r1, jnp.concatenate([high, low], 0))
        high, low = split(y2[rows])
        z += mm(r2, jnp.concatenate([high, low], 0))
        out_ref[j] += z


def rotation(gap, cross2, least):
    cross4 = cross2 * cross2
    square = gap * gap + (cross4 + 1e-37)
    root = square * lax.rsqrt(square) + tiny_value * GRAM_SCALE
    base = jnp.abs(gap) + root
    inverse = lax.rsqrt(base * base + cross4)
    signed = jnp.where(gap >= least, cross2, -cross2)
    return base * inverse, signed * inverse


def rotations(top, bottom, cross, least):
    both = [rotation(b - t, x + x, e) for t, b, x, e in zip(top, bottom, cross, least)]
    return tuple(p[0] for p in both), tuple(p[1] for p in both)


def shift(top, bottom):
    sub = lax.broadcasted_iota(jnp.int32, (8, 128), 0)
    (ta, tb), (ba, bb) = top, bottom
    down_a, down_b, first_b = pltpu.roll(ta, 1, 0), pltpu.roll(tb, 1, 0), pltpu.roll(ba, 1, 0)
    up_a, up_b = pltpu.roll(ba, 7, 0), pltpu.roll(bb, 7, 0)
    return (
        (jnp.where(sub == 0, ta, jnp.where(sub == 1, first_b, down_a)), jnp.where(sub == 0, down_a, down_b)),
        (jnp.where(sub == 7, up_b, up_a), jnp.where(sub == 7, tb, up_b)),
    )


def turn(cosine, sine, top, bottom):
    return shift(
        tuple(c * t - s * b for c, s, t, b in zip(cosine, sine, top, bottom)),
        tuple(s * t + c * b for c, s, t, b in zip(cosine, sine, top, bottom)),
    )


def dots(left, right):
    return [jnp.broadcast_to(jnp.sum(a * b, 1, keepdims=True), (8, 128)) for a, b in zip(left, right)]


def one_round(state, least):
    kt, kb, ut, ub = state
    c, s = rotations(dots(kt, ut), dots(kb, ub), dots(kt, ub), least)
    return turn(c, s, kt, kb) + turn(c, s, ut, ub)


def two_rounds(state, least, least_next):
    kt, kb, ut, ub = state
    top, bottom, cross = dots(kt, ut), dots(kb, ub), dots(kt, ub)
    kt_t, kb_t = shift(kt, kt)[0], shift(kb, kb)[0]
    ut_b, ub_b = shift(ut, ut)[1], shift(ub, ub)[1]
    quads = zip(dots(kt_t, ut_b), dots(kt_t, ub_b), dots(kb_t, ut_b), dots(kb_t, ub_b))
    c, s = rotations(top, bottom, cross, least)
    new_top, new_bottom = [], []
    for ci, si, t, b, x in zip(c, s, top, bottom, cross):
        cc, ss, mixed = ci * ci, si * si, (2.0 * ci * si) * x
        new_top.append(cc * t + ss * b - mixed)
        new_bottom.append(ss * t + cc * b + mixed)
    new_top, new_bottom = shift(new_top, new_bottom)
    of_t, of_b = shift(c, s), shift(tuple(-v for v in s), c)
    new_cross = [
        at * (ab * tt + bb * tb) + bt * (ab * bt_ + bb * bb_)
        for at, ab, bt, bb, (tt, tb, bt_, bb_) in zip(of_t[0], of_t[1], of_b[0], of_b[1], quads)
    ]
    c2, s2 = rotations(new_top, new_bottom, new_cross, least_next)
    kt, kb = turn(c2, s2, *turn(c, s, kt, kb))
    ut, ub = turn(c2, s2, *turn(c, s, ut, ub))
    return kt, kb, ut, ub


def jacobi_kernel(threshold, g_ref, h_ref, table, out_ref):
    lane = lax.broadcasted_iota(jnp.int32, (8, 128), 1)
    sub = lax.broadcasted_iota(jnp.int32, (8, 128), 0)
    gram = (g_ref[...] + h_ref[...]) * GRAM_SCALE
    rows = [gram[i : i + 1] for i in range(16)] + [gram[31 - i : 32 - i] for i in range(16)]
    k = [jnp.concatenate(rows[8 * i : 8 * i + 8], 0) for i in range(4)]
    u = [jnp.where(lane == label, 1.0, 0.0) for label in (sub, sub + 8, 31 - sub, 23 - sub)]
    state = ((k[0], k[1]), (k[2], k[3]), (u[0], u[1]), (u[2], u[3]))
    total = JSWEEPS * (ORDER - 1)

    def least(m):
        at = lax.rem(m, ORDER - 1)
        return table[at, 0:8], table[at, 8:16]

    state = lax.fori_loop(
        0, total // 2, lambda m, held: two_rounds(held, least(2 * m), least(2 * m + 1)), state, unroll=2
    )
    if total % 2:
        state = one_round(state, least(total - 1))
    kt, kb, ut, ub = state
    factors = []
    for value in dots(kt + kb, ut + ub):
        value = jnp.maximum(value * (1.0 / GRAM_SCALE), threshold * threshold)
        factors.append(1.0 - threshold / jnp.sqrt(value))
    vectors = jnp.concatenate(ut + ub, 0)
    mixing = lax.dot_general(
        jnp.concatenate(factors, 0) * vectors,
        vectors,
        (((0,), (0,)), ((), ())),
        precision=lax.Precision.HIGHEST,
        preferred_element_type=f32,
    )
    out_ref[...] = mixing[0:ORDER]


def mixing_left(where_ref, m_ref):
    own = m_ref[pl.ds(pl.multiple_of(where_ref[2] * OWN, OWN), OWN), :]
    first = own[:, 0:16]
    second = own[:, 16:32]
    zero_chan = where_ref[2] == 0
    mix = jnp.concatenate([jnp.where(zero_chan, first, second), jnp.where(zero_chan, second, first)], 1)
    high, low = split(mix)
    left = jnp.concatenate([high, high, low], 1)
    blank = jnp.zeros_like(left)
    return jnp.concatenate([jnp.concatenate([left, blank], 1), jnp.concatenate([blank, left], 1)], 0)


def apply_rows(left, own_ref, peer_ref, out_ref, first_row, count):
    for r in range(0, count, 8):
        pieces = []
        for j in range(0, 8, 2):
            stack = []
            for q in range(2):
                both = jnp.concatenate([own_ref[first_row + r + j + q], peer_ref[r + j + q]], 0)
                high, low = split(both)
                stack += [high, low, high]
            pieces.append(mm(left, jnp.concatenate(stack, 0)).reshape(2, OWN, COLS))
        block = jnp.concatenate(pieces, 0)
        for c in range(2):
            rows = slice(first_row + r, first_row + r + 8)
            out_ref[8 * c : 8 * c + 8, rows, :] = jnp.swapaxes(block[:, 8 * c : 8 * c + 8, :], 0, 1)


def apply_near(where_ref, m_ref, mine_ref, near_ref, out_ref):
    apply_rows(mixing_left(where_ref, m_ref), mine_ref, near_ref, out_ref, 0, 32)


def apply_far(where_ref, m_ref, other_ref, near_ref, far1_ref, far2_ref, done_ref, out_ref):
    left = mixing_left(where_ref, m_ref)
    apply_rows(left, other_ref, near_ref.at[32:40], out_ref, 0, 8)
    apply_rows(left, other_ref, far1_ref, out_ref, 8, 16)
    apply_rows(left, other_ref, far2_ref, out_ref, 24, 8)


FORWARD, BACKWARD = stencil_tables()
LEAST = jacobi_tables()


def whole(shape):
    return pl.BlockSpec(shape, lambda i, where, n=len(shape): (0,) * n)


def at_place(table, axis):
    return pl.BlockSpec((1, *table.shape[1:]), lambda i, where: (where[axis], 0, 0))


def call(kernel, name, where, args, outs, specs=None, out_specs=None, scratch=(), grid=1, vmem=24, us=1.0, alias=None):
    specs = specs or (None,) * len(args)
    out_specs = out_specs or (None,) * len(outs)
    return pl.pallas_call(
        kernel,
        out_shape=[jax.ShapeDtypeStruct(s, f32) for s in outs],
        grid_spec=pltpu.PrefetchScalarGridSpec(
            num_scalar_prefetch=1,
            grid=(grid,),
            in_specs=[whole(a.shape) if s is None else s for a, s in zip(args, specs)],
            out_specs=[whole(a) if s is None else s for a, s in zip(outs, out_specs)],
            scratch_shapes=list(scratch),
        ),
        compiler_params=pltpu.CompilerParams(vmem_limit_bytes=vmem * 2**20),
        cost_estimate=pl.CostEstimate(flops=0, bytes_accessed=int(us * 3.5e6), transcendentals=0),
        input_output_aliases=alias or {},
        name=name,
    )(where, *args)


def shards(x, w):
    frow, fcol, chan = (lax.axis_index(a) for a in ("frow", "fcol", "chan"))
    last_r, last_c = lax.axis_size("frow") - 1, lax.axis_size("fcol") - 1

    def place(i, last):
        return jnp.where(i == 0, 0, jnp.where(i == last, 2, 1))

    where = jnp.stack([place(frow, last_r), place(fcol, last_c), chan, frow % 2, fcol % 2]).astype(jnp.int32)
    even = [(i, i ^ 1) for i in range(8)]
    odd = [(i, i + 1) for i in range(1, 7, 2)] + [(i + 1, i) for i in range(1, 7, 2)]
    swap = [(0, 1), (1, 0)]
    tile = (2, EIN, 128)
    half = (32, OWN, COLS)
    rim = (OWN + 3, 16, COLS)
    hbm = pl.BlockSpec(memory_space=pltpu.HBM)
    (cut,) = call(
        cut_kernel, "cut", where, (x,), ((OWN, 40, COLS),), (hbm,), scratch=(pltpu.SemaphoreType.DMA((2,)),), us=0.6
    )
    near = lax.ppermute(cut, "chan", swap)
    later, _ = lax.optimization_barrier((where, cut))
    rim_e, rim_o = call(
        rim_kernel, "rim", later, (x, w), (rim, rim), (hbm, hbm), scratch=(pltpu.SemaphoreType.DMA((4,)),), us=0.6
    )
    rows_o = lax.ppermute(rim_o, "frow", odd)
    rows_e = lax.ppermute(rim_e, "frow", even)
    late, _ = lax.optimization_barrier((where, rim_e))
    side_e, side_o, mine, other = call(
        pack_kernel,
        "pack",
        late,
        (x, w),
        (tile, tile, half, half),
        (hbm, hbm),
        scratch=(pltpu.VMEM((OWN + 3, ROWS, COLS), f32), pltpu.SemaphoreType.DMA((5,))),
        us=1.5,
    )
    side_e, side_o = call(
        pack_halo_kernel, "pack_halo", where, (side_e, side_o, rows_e, rows_o), (tile, tile), us=0.7
    )
    cols_o = lax.ppermute(side_o, "fcol", odd)
    own, _ = lax.optimization_barrier((mine, side_o))
    send, near = call(gram_kernel, "gram", where, (own, near), ((ORDER, 128), (40, OWN, COLS)), us=1.2)
    side_e, _ = lax.optimization_barrier((side_e, send))
    cols_e = lax.ppermute(side_e, "fcol", even)
    got = lax.ppermute(send, "chan", swap)
    cols_e, cols_o, got = lax.optimization_barrier((cols_e, cols_o, got))
    steps = OWN // CB
    bands, totals = call(
        forward_steps,
        "forward",
        where,
        (x, rows_e, rows_o, cols_e, cols_o, FORWARD, FORWARD),
        ((OWN, 3, EOUT, WIDE), (3 * EOUT + EOUT // 2, COLS)),
        (None,) * 5 + (at_place(FORWARD, 1), at_place(FORWARD, 0)),
        (pl.BlockSpec((CB, 3, EOUT, WIDE), lambda i, where: (i, 0, 0, 0)), None),
        (
            pltpu.VMEM((CB, EOUT, WIDE), f32),
            pltpu.VMEM((2, CB * EOUT, 2 * WIDE), bf16),
            pltpu.VMEM((3, EOUT, WIDE), f32),
            pltpu.VMEM((2 * WIDE, WIDE), bf16),
            pltpu.VMEM((2 * WIDE, WIDE), bf16),
        ),
        steps,
        us=4.5,
    )
    totals_peer = lax.ppermute(totals, "chan", swap)
    part1, part2, _ = lax.optimization_barrier((mine[8:24], mine[24:32], totals))
    far1 = lax.ppermute(part1, "chan", swap)
    far2 = lax.ppermute(part2, "chan", swap)
    threshold = rank_level * math.sqrt(ROWS * COLS)
    send, _ = lax.optimization_barrier((send, totals))
    (mixing,) = call(
        lambda where_ref, *refs: jacobi_kernel(threshold, *refs),
        "jacobi",
        where,
        (send, got, LEAST),
        ((ORDER, 128),),
        us=8.5,
    )
    (low,) = call(
        apply_near,
        "apply_near",
        where,
        (mixing, mine, near),
        ((OWN, ROWS, COLS),),
        None,
        (pl.BlockSpec((OWN, 32, COLS), lambda i, where: (0, where[2], 0)),),
        us=1.2,
    )
    totals_peer, low = lax.optimization_barrier((totals_peer, low))
    (back,) = call(
        backward_kernel,
        "backward",
        where,
        (bands, totals, totals_peer, w, rows_e, rows_o, cols_e, cols_o, BACKWARD, BACKWARD),
        ((OWN, ROWS, COLS),),
        (pl.BlockSpec((CB, 3, EOUT, WIDE), lambda i, where: (i, 0, 0, 0)),)
        + (None,) * 7
        + (at_place(BACKWARD, 1), at_place(BACKWARD, 0)),
        (pl.BlockSpec((CB, ROWS, COLS), lambda i, where: (i, 0, 0)),),
        (
            pltpu.VMEM((3, EOUT, WIDE), f32),
            pltpu.VMEM((2, CB * EOUT, 2 * WIDE), bf16),
            pltpu.VMEM((2 * WIDE, COLS), bf16),
            pltpu.VMEM((2 * WIDE, COLS), bf16),
        ),
        steps,
        us=4.5,
    )
    low, back = lax.optimization_barrier((low, back))
    (low,) = call(
        apply_far,
        "apply_far",
        where,
        (mixing, other, near, far1, far2, low),
        ((OWN, ROWS, COLS),),
        (None,) * 5 + (hbm,),
        (pl.BlockSpec((OWN, 32, COLS), lambda i, where: (0, 1 - where[2], 0)),),
        us=1.2,
        alias={6: 0},
    )
    return back, low


def solution(mesh):
    return jax.shard_map(
        shards,
        mesh=mesh,
        in_specs=(P("chan", "frow", "fcol"), P(None, "frow", "fcol")),
        out_specs=(P("chan", "frow", "fcol"), P("chan", "frow", "fcol")),
        check_vma=False,
    )
```
